32 devices in a mesh: dp: 8 (over y, x, core), tp: 4 (over z).
Axes of the slice: x: 2, y: 2, z: 4, core: 2. Of those that a mesh axis runs over, the one named last changes fastest.
Arguments:
- tokens: bfloat16 [16, 2048, 768], P('dp', 'tp'), may hold values from -6 to 6
- segment_ids: int32 [16, 2048], P('dp'), may hold values from 0 to 65535, as said below
- positions: int32 [16, 2048], P('dp'), may hold values from 0 to 2015, as said below
- w_qkv: bfloat16 [768, 2304], P(None, ('dp', 'tp')), may hold values from -0.3125 to 0.3125
- w_out: bfloat16 [768, 768], P(None, ('dp', 'tp')), may hold values from -0.875 to 0.875
- norm1_gain: bfloat16 [768], P(('dp', 'tp')), may hold values from 0.5 to 1.5
- norm1_shift: bfloat16 [768], P(('dp', 'tp')), may hold values from -1.5 to 1.5
- w_gate: bfloat16 [768, 3072], P('dp', 'tp'), may hold values from -0.21875 to 0.21875
- w_up: bfloat16 [768, 3072], P('dp', 'tp'), may hold values from -0.21875 to 0.21875
- w_down: bfloat16 [3072, 768], P('tp', 'dp'), may hold values from -0.15625 to 0.15625
- norm2_gain: bfloat16 [768], P(('dp', 'tp')), may hold values from 0.5 to 1.5
- norm2_shift: bfloat16 [768], P(('dp', 'tp')), may hold values from -1.5 to 1.5
- out_grad: bfloat16 [16, 2048, 768], P('dp', 'tp'), may hold values from -6 to 6
Outputs:
- output: bfloat16 [16, 2048, 768], P('dp', 'tp')
- in_grad: bfloat16 [16, 2048, 768], P('dp', 'tp')
- g_qkv: float32 [768, 2304], P(None, ('dp', 'tp'))
- g_out: float32 [768, 768], P(None, ('dp', 'tp'))
- g_norm1_gain: float32 [768], P(('dp', 'tp'))
- g_norm1_shift: float32 [768], P(('dp', 'tp'))
- g_gate: float32 [768, 3072], P('dp', 'tp')
- g_up: float32 [768, 3072], P('dp', 'tp')
- g_down: float32 [3072, 768], P('tp', 'dp')
- g_norm2_gain: float32 [768], P(('dp', 'tp'))
- g_norm2_shift: float32 [768], P(('dp', 'tp'))
The draws below stay inside these ranges and needn't reach their ends.
Inputs may be any that keep to these rules, and one draw needn't show every extreme that they name: `segment_ids`: in each row the tokens of a document are contiguous and share an id, and the row's two documents have different ids: the first starts at slot 0 and the second fills the last t slots, t from 32 to 64, drawn for each row. Each document's positions count 0, 1, 2, ... from its first token.
All inputs are finite; a program needn't handle non-finite values.
Results may differ from the reference program's by a relative error of at most 0.02.
The reference program's roundings to bfloat16 on the way count: a program that leaves them out, or rounds other values in their place, can miss the bound.
Values may be sent and summed in bfloat16 or wider, within the bound.
No kernel may reach another device: no remote copies, remote signals or barrier semaphores. Data moves between devices by JAX's collectives and lax.ppermute only.
A program may use at most 384 MiB of HBM per device.

```python
import jax
import jax.numpy as jnp
from jax import lax

D = 768
HEADS = 12
HEAD_DIM = 64
FF = 3072
SEQ = 2048
ROWS = 16


def layout(key):
    tail_sizes = jax.random.randint(jax.random.fold_in(key, 11), (ROWS, 1), SEQ // 64, SEQ // 32 + 1)
    first_id = jax.random.randint(jax.random.fold_in(key, 12), (ROWS, 1), 0, 32768)
    chosen_row = jax.random.randint(jax.random.fold_in(key, 14), (), 0, ROWS)
    row_index = jnp.arange(ROWS, dtype=jnp.int32)[:, None]
    is_chosen = row_index == chosen_row
    tail_sizes = jnp.where(is_chosen, SEQ // 64, tail_sizes)
    first_id = jnp.where(is_chosen, 0, first_id)
    second_id = 65535 - first_id
    slot_index = jnp.arange(SEQ, dtype=jnp.int32)[None, :]
    tail_start = SEQ - tail_sizes
    in_tail = slot_index >= tail_start
    doc_ids = jnp.where(in_tail, second_id, first_id)
    doc_places = jnp.where(in_tail, slot_index - tail_start, slot_index)
    return (doc_ids.astype(jnp.int32), doc_places.astype(jnp.int32))


def draw_segment_ids(key, part):
    return layout(key)[0]


def draw_positions(key, part):
    return layout(key)[1]


def steps_of(rng, dims, cuts, smallest, largest):
    factor_of, own = 1.0, jax.random.fold_in(rng, 6)
    for position, blocks in cuts:
        draws = jnp.exp(jax.random.uniform(jax.random.fold_in(own, position), (blocks,), jnp.float32, smallest / len(cuts), largest / len(cuts)))
        factor_of = factor_of * jnp.repeat(draws, dims[position] // blocks).reshape([-1 if axis == position else 1 for axis in range(len(dims))])
    return factor_of


def noise(stream_key, extent, deviation, limit, cuts=(), held_as=jnp.bfloat16):
    entries = deviation * jax.random.normal(stream_key, extent, jnp.float32)
    if cuts:
        entries = entries * steps_of(stream_key, extent, cuts, -0.22, 0.18)
    return jnp.clip(entries, -limit, limit).astype(held_as)


def setup_inputs(seed: int = 0) -> dict:
    streams_of = jax.random.split(jax.random.key(seed), 14)
    tokens = noise(streams_of[0], (ROWS, SEQ, D), 1.0, 6.0, ((0, 8), (1, 4)))
    segment_ids = draw_segment_ids(jax.random.fold_in(streams_of[13], 71), 0)
    positions = draw_positions(jax.random.fold_in(streams_of[13], 71), 0)
    w_qkv = noise(streams_of[3], (D, 3 * D), (D // 2) ** -0.5, 0.3125, ((1, 32),))
    w_out = noise(streams_of[4], (D, D), (D // 16) ** -0.5, 0.875, ((1, 32),))
    norm1_gain = jnp.clip(1.0 + 0.1 * jax.random.normal(streams_of[5], (D,), jnp.float32), 0.5, 1.5).astype(jnp.bfloat16)
    norm1_shift = noise(streams_of[6], (D,), 0.3, 1.5, ((0, 32),))
    w_gate = noise(streams_of[7], (D, FF), D ** -0.5, 0.21875, ((0, 8), (1, 4)))
    w_up = noise(streams_of[8], (D, FF), D ** -0.5, 0.21875, ((0, 8), (1, 4)))
    w_down = noise(streams_of[9], (FF, D), (FF // 2) ** -0.5, 0.15625, ((0, 4), (1, 8)))
    norm2_gain = jnp.clip(1.0 + 0.1 * jax.random.normal(streams_of[10], (D,), jnp.float32), 0.5, 1.5).astype(jnp.bfloat16)
    norm2_shift = noise(streams_of[11], (D,), 0.3, 1.5, ((0, 32),))
    out_grad = noise(streams_of[12], (ROWS, SEQ, D), 1.0, 6.0, ((0, 8), (1, 4)))
    return {"tokens": tokens, "segment_ids": segment_ids, "positions": positions, "w_qkv": w_qkv, "w_out": w_out, "norm1_gain": norm1_gain, "norm1_shift": norm1_shift, "w_gate": w_gate, "w_up": w_up, "w_down": w_down, "norm2_gain": norm2_gain, "norm2_shift": norm2_shift, "out_grad": out_grad}


@jax.custom_vjp
def low(v):
    return lax.optimization_barrier(v.astype(jnp.bfloat16)).astype(jnp.float32)

@jax.custom_vjp
def low_back(v):
    return v

def low_keep(v):
    return (low(v), None)

def low_pass(kept, grad):
    return (grad,)

def back_keep(v):
    return (v, None)

def back_low(kept, grad):
    return (low(grad),)
low.defvjp(low_keep, low_pass)
low_back.defvjp(back_keep, back_low)
EPSILON = 1e-05

def rope_tables(positions):
    half_dim = HEAD_DIM // 2
    frequency = 1000.0 ** (-(jnp.arange(half_dim, dtype=jnp.float32) * 2.0) / HEAD_DIM)
    angles = positions.astype(jnp.float32)[..., None] * frequency
    return (jnp.cos(angles), jnp.sin(angles))

def rotate(values, cosine, sine):
    half_dim = values.shape[-1] // 2
    front = values[..., :half_dim]
    behind = values[..., half_dim:]
    cos_part = cosine[..., None, :]
    sin_part = sine[..., None, :]
    return jnp.concatenate([front * cos_part - behind * sin_part, behind * cos_part + front * sin_part], axis=-1)

def normalize(values, gain, shift):
    center = lax.optimization_barrier(jnp.mean(values, axis=-1, keepdims=True))
    centered = values - center
    variance = lax.optimization_barrier(jnp.mean(centered * centered, axis=-1, keepdims=True))
    return centered * lax.rsqrt(variance + EPSILON) * gain + shift

def attend_row(row_items):
    queries, keys, values, segments = row_items
    scores = jnp.einsum('qhd,khd->hqk', queries, keys, precision=lax.Precision.HIGHEST) * HEAD_DIM ** (-0.5)
    scores = low_back(scores)
    same_doc = segments[:, None] == segments[None, :]
    scores = jnp.where(same_doc[None], scores, -1e+30)
    row_top = lax.optimization_barrier(jnp.max(scores, axis=-1, keepdims=True))
    expo_terms = jnp.exp(scores - row_top)
    soft_probs = low(expo_terms / lax.optimization_barrier(jnp.sum(expo_terms, axis=-1, keepdims=True)))
    return jnp.einsum('hqk,khd->qhd', soft_probs, values, precision=lax.Precision.HIGHEST)

def forward(params, segment_ids, cosine, sine):
    tokens, w_qkv, w_out, norm1_gain, norm1_shift, w_gate, w_up, w_down, norm2_gain, norm2_shift = params
    row_count, seq_len, width = tokens.shape
    head_shape = (row_count, seq_len, HEADS, HEAD_DIM)
    joined = low_back(jnp.einsum('rsd,de->rse', tokens, w_qkv, precision=lax.Precision.HIGHEST))
    queries = low(rotate(joined[..., :width].reshape(head_shape), cosine, sine))
    keys = low(rotate(joined[..., width:2 * width].reshape(head_shape), cosine, sine))
    values = low(joined[..., 2 * width:].reshape(head_shape))
    attended = lax.map(jax.checkpoint(attend_row), (queries, keys, values, segment_ids))
    attended = low(low_back(attended.reshape(row_count, seq_len, width)))
    projected = low_back(jnp.einsum('rsd,de->rse', attended, w_out, precision=lax.Precision.HIGHEST))
    hidden_in = normalize(tokens + projected, norm1_gain, norm1_shift)
    mlp_in = low(hidden_in)
    gate = low_back(jnp.einsum('rsd,df->rsf', mlp_in, w_gate, precision=lax.Precision.HIGHEST))
    up_part = low_back(jnp.einsum('rsd,df->rsf', mlp_in, w_up, precision=lax.Precision.HIGHEST))
    hidden = low(jax.nn.silu(gate) * up_part)
    mixed = low_back(jnp.einsum('rsf,fd->rsd', hidden, w_down, precision=lax.Precision.HIGHEST))
    return normalize(hidden_in + mixed, norm2_gain, norm2_shift)

def reference(tokens, segment_ids, positions, w_qkv, w_out, norm1_gain, norm1_shift, w_gate, w_up, w_down, norm2_gain, norm2_shift, out_grad):
    cosine, sine = rope_tables(positions)
    floats = tuple((array_in.astype(jnp.float32) for array_in in (tokens, w_qkv, w_out, norm1_gain, norm1_shift, w_gate, w_up, w_down, norm2_gain, norm2_shift)))

    def layer(params):
        return forward(params, segment_ids, cosine, sine)
    output, pullback = jax.vjp(layer, floats)
    grads = pullback(out_grad.astype(jnp.float32))[0]
    return (output.astype(jnp.bfloat16), grads[0].astype(jnp.bfloat16), grads[1], grads[2], grads[3], grads[4], grads[5], grads[6], grads[7], grads[8], grads[9])
```

```python
import functools

import jax
import jax.numpy as jnp
from jax import lax
from jax.experimental import pallas as pl
from jax.experimental.pallas import tpu as pltpu
from jax.sharding import Mesh, PartitionSpec as P

HEADS = 12
HEAD_DIM = 64
EPSILON = 1e-05
AUG = 16
MASK = 2.0**99
LOW = jnp.bfloat16
WIDE = jnp.float32
SWAP = [(0, 1), (1, 0)]


def dot(a, b, ca, cb):
    return lax.dot_general(a, b, (((ca,), (cb,)), ((), ())), preferred_element_type=WIDE)


def split3(x):
    high = x.astype(LOW)
    rest = x - high.astype(WIDE)
    middle = rest.astype(LOW)
    return [high, middle, (rest - middle.astype(WIDE)).astype(LOW)]


def put_rows(base, at, rows):
    index = lax.broadcasted_iota(jnp.int32, base.shape, 0)
    out = base.astype(WIDE)
    for i, row in enumerate(rows):
        out = jnp.where(index == at + i, row.astype(WIDE), out)
    return out.astype(LOW)


def ones_row(n):
    return jnp.ones((1, n), WIDE)


def forward_kernel(parts, *refs):
    q_ref, qa_ref = refs[:2]
    k_refs, v_refs, ka_refs = refs[2 : 2 + parts], refs[2 + parts : 2 + 2 * parts], refs[2 + 2 * parts : 2 + 3 * parts]
    o_ref, lse_ref, keys = refs[2 + 3 * parts :]
    at = 0
    values = []
    for k_ref, v_ref, ka_ref in zip(k_refs, v_refs, ka_refs):
        n = k_ref.shape[1]
        keys[at : at + n] = jnp.concatenate([k_ref[...], ka_ref[...]], axis=0).T
        values.append(v_ref[...])
        at += n
    queries = jnp.concatenate([q_ref[...], qa_ref[...]], axis=0)
    scores = dot(keys[...], queries, 1, 0)
    top = jnp.max(scores, axis=0, keepdims=True)
    terms = jnp.exp(scores - top)
    total = jnp.sum(terms, axis=0, keepdims=True)
    result = dot(jnp.concatenate(values, axis=1), terms.astype(LOW), 1, 0)
    o_ref[...] = (result / total).astype(LOW)
    lse_ref[...] = (top + jnp.log(total)).reshape(1, 1, -1)


def attend_forward(q, qa, ks, vs, kas):
    parts, nq = len(ks), q.shape[1]
    nk = sum(k.shape[1] for k in ks)
    head = lambda n: pl.BlockSpec((HEAD_DIM, n), lambda h: (h, 0))
    whole = lambda n: pl.BlockSpec((AUG, n), lambda h: (0, 0))
    return pl.pallas_call(
        functools.partial(forward_kernel, parts),
        grid=(HEADS,),
        in_specs=[head(nq), whole(nq)]
        + [head(k.shape[1]) for k in ks]
        + [head(v.shape[1]) for v in vs]
        + [whole(k.shape[1]) for k in ks],
        out_specs=[head(nq), pl.BlockSpec((1, 1, nq), lambda h: (h, 0, 0))],
        out_shape=[
            jax.ShapeDtypeStruct((HEADS * HEAD_DIM, nq), LOW),
            jax.ShapeDtypeStruct((HEADS, 1, nq), WIDE),
        ],
        scratch_shapes=[pltpu.VMEM((nk, HEAD_DIM + AUG), LOW)],
        compiler_params=pltpu.CompilerParams(vmem_limit_bytes=56 << 20),
        cost_estimate=pl.CostEstimate(
            flops=16 * HEADS * nq * nk * HEAD_DIM, bytes_accessed=4 * HEADS * HEAD_DIM * (nq + nk), transcendentals=HEADS * nq * nk
        ),
        name="attend_forward",
    )(q, qa, *ks, *vs, *kas)


def backward_kernel(parts, *refs):
    q_ref, g_ref, o_ref, lse_ref, qa_ref = refs[:5]
    k_refs, v_refs, ka_refs = refs[5 : 5 + parts], refs[5 + parts : 5 + 2 * parts], refs[5 + 2 * parts : 5 + 3 * parts]
    dq_ref = refs[5 + 3 * parts]
    dk_refs = refs[6 + 3 * parts : 6 + 4 * parts]
    dv_refs = refs[6 + 4 * parts : 6 + 5 * parts]
    keys, values = refs[6 + 5 * parts :]
    nq = q_ref.shape[1]
    at = 0
    key_list = []
    for k_ref, v_ref, ka_ref in zip(k_refs, v_refs, ka_refs):
        n = k_ref.shape[1]
        keys[at : at + n] = jnp.concatenate(
            [k_ref[...], put_rows(ka_ref[...], 2, [ones_row(n)] * 3)], axis=0
        ).T
        values[at : at + n] = jnp.concatenate(
            [v_ref[...], put_rows(jnp.zeros((AUG, n), LOW), 0, [ones_row(n)] * 3)], axis=0
        ).T
        key_list.append(k_ref[...])
        at += n
    grads, queries = g_ref[...], q_ref[...]
    delta = jnp.sum(grads.astype(WIDE) * o_ref[...].astype(WIDE), axis=0, keepdims=True)
    query_aug = jnp.concatenate([queries, put_rows(qa_ref[...], 2, split3(-lse_ref[0]))], axis=0)
    grad_aug = jnp.concatenate([grads, put_rows(jnp.zeros((AUG, nq), LOW), 0, split3(-delta))], axis=0)
    probs = jnp.exp(dot(keys[...], query_aug, 1, 0))
    prob_grads = dot(values[...], grad_aug, 1, 0)
    low_probs = probs.astype(LOW)
    score_grads = (probs * prob_grads).astype(LOW)
    dq_ref[...] = dot(jnp.concatenate(key_list, axis=1), score_grads, 1, 0) * HEAD_DIM ** (-0.5)
    dv = dot(grads, low_probs, 1, 1)
    dk = dot(queries, score_grads, 1, 1)
    at = 0
    for dk_ref, dv_ref in zip(dk_refs, dv_refs):
        n = dk_ref.shape[1]
        dk_ref[...] = dk[:, at : at + n].astype(dk_ref.dtype)
        dv_ref[...] = dv[:, at : at + n].astype(dv_ref.dtype)
        at += n


def attend_backward(q, g, o, lse, qa, ks, vs, kas, types):
    parts, nq = len(ks), q.shape[1]
    sizes = [k.shape[1] for k in ks]
    nk = sum(sizes)
    head = lambda n: pl.BlockSpec((HEAD_DIM, n), lambda h: (h, 0))
    whole = lambda n: pl.BlockSpec((AUG, n), lambda h: (0, 0))
    width = HEADS * HEAD_DIM
    out = pl.pallas_call(
        functools.partial(backward_kernel, parts),
        grid=(HEADS,),
        in_specs=[head(nq), head(nq), head(nq), pl.BlockSpec((1, 1, nq), lambda h: (h, 0, 0)), whole(nq)]
        + [head(n) for n in sizes]
        + [head(n) for n in sizes]
        + [whole(n) for n in sizes],
        out_specs=[head(nq)] + [head(n) for n in sizes] * 2,
        out_shape=[jax.ShapeDtypeStruct((width, nq), WIDE)]
        + [jax.ShapeDtypeStruct((width, n), t) for n, t in zip(sizes, types)] * 2,
        scratch_shapes=[pltpu.VMEM((nk, HEAD_DIM + AUG), LOW)] * 2,
        compiler_params=pltpu.CompilerParams(vmem_limit_bytes=60 << 20),
        cost_estimate=pl.CostEstimate(
            flops=30 * HEADS * nq * nk * HEAD_DIM, bytes_accessed=8 * width * (nq + nk), transcendentals=HEADS * nq * nk
        ),
        name="attend_backward",
    )(q, g, o, lse, qa, *ks, *vs, *kas)
    return out[0], out[1 : 1 + parts], out[1 + parts :]


def norm_forward(values, gain, shift):
    center = jnp.mean(values, axis=-1, keepdims=True)
    centered = values - center
    inverse = lax.rsqrt(jnp.mean(centered * centered, axis=-1, keepdims=True) + EPSILON)
    normed = centered * inverse
    return (normed * gain + shift, normed, inverse)


def norm_backward(grads, normed, inverse, gain):
    scaled = grads * gain
    first_mean = jnp.mean(scaled, axis=-1, keepdims=True)
    second_mean = jnp.mean(scaled * normed, axis=-1, keepdims=True)
    return inverse * (scaled - first_mean - normed * second_mean)


def local(
    tp, ways, tokens, segment_ids, positions, w_qkv, w_out, norm1_gain, norm1_shift, w_gate, w_up, w_down, norm2_gain, norm2_shift, out_grad
):
    rows, piece, width = tokens.shape
    chips, per_group = ways
    dp, near = 2 * chips, tp // per_group
    line = ("core", "zg", "zm")
    everyone = ("zg", "zm", "chip", "core")
    core = lax.axis_index("core")
    group = lax.axis_index("zg")
    z = group * near + lax.axis_index("zm")
    member = lax.axis_index("zm") * 2 + core
    own = rows * piece

    def ring(step):
        pairs = []
        for c in range(2):
            for j in range(tp):
                row = c * rows + (j + step) % rows
                m = j // rows
                pairs.append((c * tp + j, (m % 2) * tp + row * near + m // 2))
        return pairs

    def bring(x):
        return [
            lax.ppermute(lax.dynamic_index_in_dim(x, (z + k) % rows, 0, False), line, ring(k))
            for k in range(rows)
        ]

    def give_back(x):
        back = [
            lax.ppermute(x[k * piece : (k + 1) * piece], line, [(b, a) for a, b in ring(k)])
            for k in range(rows)
        ]
        return jnp.roll(jnp.stack(back), z, axis=0)

    def gather_all(x):
        whole = lax.all_gather(x, everyone, axis=0, tiled=False)
        return whole.reshape((tp, dp) + x.shape)

    def scatter_all(x):
        return lax.psum_scatter(
            x.reshape((tp * dp,) + x.shape[2:]).astype(LOW), everyone, scatter_dimension=0, tiled=False
        ).astype(WIDE)

    nq, no = w_qkv.shape[1], w_out.shape[1]
    pad = -(nq + no + 1) % 16
    norm_row = jnp.concatenate([norm1_gain, norm1_shift, norm2_gain, norm2_shift])
    first = jnp.concatenate(
        [w_qkv.T, w_out.T, jnp.pad(norm_row, (0, width - 4 * no))[None], jnp.zeros((pad, width), LOW)]
    )
    x = jnp.concatenate(bring(tokens))
    first = gather_all(first)
    gate_full = gather_all(w_gate).reshape(tp, width, -1)
    up_full = gather_all(w_up).reshape(tp, width, -1)
    down_full = gather_all(w_down.T).reshape(tp, width, -1)
    by_column = first.swapaxes(0, 1)
    qkv_t = by_column[:, :, :nq].reshape(3 * width, width)
    out_t = by_column[:, :, nq : nq + no].reshape(width, width)
    vectors = by_column[:, :, nq + no, : 4 * no].reshape(dp * tp, 4, no).swapaxes(0, 1).reshape(4, width)
    gain_one, shift_one, gain_two, shift_two = vectors.astype(WIDE)
    grad_top = jnp.concatenate(bring(out_grad)).astype(WIDE)

    info = jnp.stack([segment_ids, positions])
    other = lax.ppermute(info, "core", SWAP)
    info = jnp.where(core == 0, jnp.stack([info, other], 1), jnp.stack([other, info], 1))
    info = info.reshape(2, 2 * rows, -1)
    info = lax.dynamic_index_in_dim(info, group, 1, False)
    second = (info[0] != info[0, 0]).reshape(-1, rows, piece)
    second = jnp.roll(second[:, ::-1], group + 1, axis=1).reshape(-1, own)
    places = info[1].reshape(-1, rows, piece)
    places = jnp.roll(places[:, ::-1], group + 1, axis=1).reshape(-1, own)
    own_second = lax.dynamic_index_in_dim(second, member, 0, False)
    own_places = lax.dynamic_index_in_dim(places, member, 0, False)

    def key_aug(is_second):
        return jnp.pad(
            jnp.stack([jnp.where(is_second, 0.0, -MASK), jnp.where(is_second, -MASK, 0.0)]), ((0, AUG - 2), (0, 0))
        ).astype(LOW)

    query_aug = jnp.pad(
        jnp.stack([own_second, ~own_second]).astype(WIDE), ((0, AUG - 2), (0, 0))
    ).astype(LOW)

    half = HEAD_DIM // 2
    frequency = 1000.0 ** (-(jnp.arange(half, dtype=WIDE) * 2.0) / HEAD_DIM)
    angles = own_places.astype(WIDE)[None] * frequency[:, None]
    cosine, sine = jnp.cos(angles), jnp.sin(angles)

    qkv = dot(qkv_t, x, 1, 1)
    pairs = qkv[: 2 * width].reshape(2 * HEADS, 2, half, own)
    front, behind = pairs[:, 0], pairs[:, 1]
    turned = jnp.stack([front * cosine - behind * sine, behind * cosine + front * sine], axis=1)
    turned = turned.reshape(2 * width, own)
    q = (turned[:width].astype(LOW) * HEAD_DIM ** (-0.5)).astype(LOW)
    kv = jnp.concatenate([turned[width:].astype(LOW), qkv[2 * width :].astype(LOW)])
    members = 2 * near
    if members == 2:
        other_kv = lax.ppermute(kv, "core", SWAP)
        ks, vs = [kv[:width], other_kv[:width]], [kv[width:], other_kv[width:]]
        other_second = lax.dynamic_index_in_dim(second, 1 - member, 0, False)
        kas = [key_aug(own_second), key_aug(other_second)]
        types = [WIDE, LOW]
    else:
        all_kv = lax.all_gather(kv, ("zm", "core"), axis=1, tiled=True)
        ks, vs, kas = [all_kv[:width]], [all_kv[width:]], [key_aug(second.reshape(-1))]
        types = [LOW]
    attended, lse = attend_forward(q, query_aug, ks, vs, kas)

    projected = dot(attended, out_t, 0, 1)
    x_one, normed_one, inverse_one = norm_forward(x.astype(WIDE) + projected, gain_one, shift_one)
    x_low = x_one.astype(LOW)
    gate = jnp.einsum("td,jdf->jtf", x_low, gate_full, preferred_element_type=WIDE)
    up = jnp.einsum("td,jdf->jtf", x_low, up_full, preferred_element_type=WIDE)
    sigma = jax.nn.sigmoid(gate)
    activated = gate * sigma
    hidden = (activated * up).astype(LOW)
    mixed = jnp.einsum("jtf,jdf->td", hidden, down_full, preferred_element_type=WIDE)
    result, normed_two, inverse_two = norm_forward(x_one + mixed, gain_two, shift_two)
    output = give_back(result.astype(LOW))

    gain_two_grad = jnp.sum(grad_top * normed_two, axis=0)
    shift_two_grad = jnp.sum(grad_top, axis=0)
    d_resid_two = norm_backward(grad_top, normed_two, inverse_two, gain_two)
    mix_grad = d_resid_two.astype(LOW)
    hidden_grad = jnp.einsum("td,jdf->jtf", mix_grad, down_full, preferred_element_type=WIDE)
    gate_grad = (hidden_grad * up * (sigma * (1.0 + gate * (1.0 - sigma)))).astype(LOW)
    up_grad = (hidden_grad * activated).astype(LOW)
    x_terms = jnp.einsum("jtf,jdf->td", gate_grad, gate_full, preferred_element_type=WIDE)
    x_terms = x_terms + jnp.einsum("jtf,jdf->td", up_grad, up_full, preferred_element_type=WIDE)
    d_x_one = d_resid_two + x_terms

    def weight_grad(a, b):
        full = jnp.einsum("td,jtf->jdf", a, b, preferred_element_type=WIDE)
        return scatter_all(full.reshape(tp, dp, width // dp, -1))

    g_down = weight_grad(mix_grad, hidden).T
    g_gate = weight_grad(x_low, gate_grad)
    g_up = weight_grad(x_low, up_grad)

    gain_one_grad = jnp.sum(d_x_one * normed_one, axis=0)
    shift_one_grad = jnp.sum(d_x_one, axis=0)
    d_resid_one = norm_backward(d_x_one, normed_one, inverse_one, gain_one)
    proj_grad = d_resid_one.astype(LOW)
    g_out = dot(proj_grad, attended, 0, 1)
    att_grad = dot(out_t, proj_grad, 0, 1).astype(LOW)
    dq, dks, dvs = attend_backward(q, att_grad, attended, lse, query_aug, ks, vs, kas, types)
    if members == 2:
        sent = lax.ppermute(jnp.concatenate([dks[1], dvs[1]]), "core", SWAP)
        dk = dks[0] + sent[:width].astype(WIDE)
        dv = dvs[0] + sent[width:].astype(WIDE)
    else:
        summed = lax.psum_scatter(
            jnp.concatenate([dks[0], dvs[0]]), ("zm", "core"), scatter_dimension=1, tiled=True
        ).astype(WIDE)
        dk, dv = summed[:width], summed[width:]
    pairs = jnp.concatenate([dq, dk]).reshape(2 * HEADS, 2, half, own)
    front, behind = pairs[:, 0], pairs[:, 1]
    turned = jnp.stack([front * cosine + behind * sine, behind * cosine - front * sine], axis=1)
    qkv_grad = jnp.concatenate([turned.reshape(2 * width, own), dv]).astype(LOW)
    g_qkv = dot(qkv_grad, x, 1, 0)
    in_grad = (d_resid_one + dot(qkv_grad, qkv_t, 0, 0)).astype(LOW)
    in_grad = give_back(in_grad)

    norms = jnp.stack([gain_one_grad, shift_one_grad, gain_two_grad, shift_two_grad])
    norms = norms.reshape(4, dp * tp, no).swapaxes(0, 1).reshape(dp, tp, 1, 4 * no)
    norms = jnp.pad(norms, ((0, 0), (0, 0), (0, pad), (0, width - 4 * no)))
    last = jnp.concatenate([g_qkv.reshape(dp, tp, nq, width), g_out.reshape(dp, tp, no, width), norms], axis=2)
    last = scatter_all(last.swapaxes(0, 1))
    vectors = last[nq + no, : 4 * no].reshape(4, no)
    return (
        output,
        in_grad,
        last[:nq].T,
        last[nq : nq + no].T,
        vectors[0],
        vectors[1],
        g_gate,
        g_up,
        g_down,
        vectors[2],
        vectors[3],
    )


def solution(mesh):
    dp, tp = mesh.shape["dp"], mesh.shape["tp"]

    def run(*arrays):
        rows = arrays[0].shape[0] // dp
        groups = 2 * rows
        grid = Mesh(
            mesh.devices.reshape(dp // 2, 2, groups, tp // groups), ("chip", "core", "zg", "zm")
        )
        d, t = ("chip", "core"), ("zg", "zm")
        both = d + t
        placed = (
            P(d, t, None),
            P(d, None),
            P(d, None),
            P(None, both),
            P(None, both),
            P(both),
            P(both),
            P(d, t),
            P(d, t),
            P(t, d),
            P(both),
            P(both),
            P(d, t, None),
        )
        return jax.shard_map(
            functools.partial(local, tp, (dp // 2, groups)),
            mesh=grid,
            in_specs=placed,
            out_specs=(
                P(d, t, None),
                P(d, t, None),
                P(None, both),
                P(None, both),
                P(both),
                P(both),
                P(d, t),
                P(d, t),
                P(t, d),
                P(both),
                P(both),
            ),
            check_vma=False,
        )(*arrays)

    return run
```

```python
import functools

import jax
import jax.numpy as jnp
from jax import lax
from jax.experimental import pallas as pl
from jax.experimental.pallas import tpu as pltpu
import numpy as np
from jax.sharding import Mesh, PartitionSpec as P

HEADS = 12
HEAD_DIM = 64
EPSILON = 1e-05
AUG = 16
PIECES = 4
COST = 16
MASK = 2.0**99
LOW = jnp.bfloat16
WIDE = jnp.float32
SWAP = [(0, 1), (1, 0)]


def dot(a, b, ca, cb):
    return lax.dot_general(a, b, (((ca,), (cb,)), ((), ())), preferred_element_type=WIDE)


def cost(flops=0, bytes_accessed=0, transcendentals=0, scale=COST):
    return pl.CostEstimate(
        flops=flops // scale, bytes_accessed=bytes_accessed // scale, transcendentals=transcendentals // scale
    )


def split3(x):
    high = x.astype(LOW)
    rest = x - high.astype(WIDE)
    middle = rest.astype(LOW)
    return [high, middle, (rest - middle.astype(WIDE)).astype(LOW)]


def put_rows(base, at, rows):
    index = lax.broadcasted_iota(jnp.int32, base.shape, 0)
    out = base.astype(WIDE)
    for i, row in enumerate(rows):
        out = jnp.where(index == at + i, row.astype(WIDE), out)
    return out.astype(LOW)


def ones_row(n):
    return jnp.ones((1, n), WIDE)


def forward_kernel(parts, *refs):
    q_ref, qa_ref = refs[:2]
    refs = refs[: 2 + 3 * parts] + refs[-3:]
    k_refs, v_refs, ka_refs = refs[2 : 2 + parts], refs[2 + parts : 2 + 2 * parts], refs[2 + 2 * parts : 2 + 3 * parts]
    o_ref, lse_ref, keys = refs[2 + 3 * parts :]
    at = 0
    values = []
    for k_ref, v_ref, ka_ref in zip(k_refs, v_refs, ka_refs):
        n = k_ref.shape[1]
        keys[at : at + n] = jnp.concatenate([k_ref[...], ka_ref[...]], axis=0).T
        values.append(v_ref[...])
        at += n
    queries = jnp.concatenate([q_ref[...], qa_ref[...]], axis=0)
    scores = dot(keys[...], queries, 1, 0)
    top = jnp.max(scores, axis=0, keepdims=True)
    terms = jnp.exp(scores - top)
    total = jnp.sum(terms, axis=0, keepdims=True)
    result = dot(jnp.concatenate(values, axis=1), terms.astype(LOW), 1, 0)
    o_ref[...] = (result / total).astype(LOW)
    lse_ref[...] = (top + jnp.log(total)).reshape(1, 1, -1)


def head_block(n, first):
    return pl.BlockSpec((HEAD_DIM, n), lambda h: (h + first, 0))


def whole_block(rows, n):
    return pl.BlockSpec((rows, n), lambda h: (0, 0))


def attend_forward(q, qa, kvs, kas, after, first, heads):
    parts, nq = len(kvs), q.shape[1]
    sizes = [kv.shape[1] for kv in kvs]
    nk = sum(sizes)
    return pl.pallas_call(
        functools.partial(forward_kernel, parts),
        grid=(heads,),
        in_specs=[head_block(nq, first), whole_block(AUG, nq)]
        + [head_block(n, first) for n in sizes]
        + [head_block(n, first + HEADS) for n in sizes]
        + [whole_block(AUG, n) for n in sizes]
        + [pl.BlockSpec(memory_space=pl.ANY)] * len(after),
        out_specs=[head_block(nq, 0), pl.BlockSpec((1, 1, nq), lambda h: (h, 0, 0))],
        out_shape=[
            jax.ShapeDtypeStruct((heads * HEAD_DIM, nq), LOW),
            jax.ShapeDtypeStruct((heads, 1, nq), WIDE),
        ],
        scratch_shapes=[pltpu.VMEM((nk, HEAD_DIM + AUG), LOW)],
        compiler_params=pltpu.CompilerParams(vmem_limit_bytes=56 << 20),
        cost_estimate=cost(
            flops=16 * heads * nq * nk * HEAD_DIM,
            bytes_accessed=4 * heads * HEAD_DIM * (nq + nk),
            transcendentals=heads * nq * nk,
        ),
        name="attend_forward",
    )(q, qa, *kvs, *kvs, *kas, *after)


def backward_kernel(parts, *refs):
    q_ref, g_ref, o_ref, lse_ref, qa_ref = refs[:5]
    refs = refs[: 5 + 3 * parts] + refs[-3 - parts :]
    k_refs, v_refs, ka_refs = refs[5 : 5 + parts], refs[5 + parts : 5 + 2 * parts], refs[5 + 2 * parts : 5 + 3 * parts]
    dq_ref = refs[5 + 3 * parts]
    dkv_refs = refs[6 + 3 * parts : 6 + 4 * parts]
    keys, values = refs[6 + 4 * parts :]
    nq = q_ref.shape[1]
    at = 0
    key_list = []
    for k_ref, v_ref, ka_ref in zip(k_refs, v_refs, ka_refs):
        n = k_ref.shape[1]
        keys[at : at + n] = jnp.concatenate(
            [k_ref[...], put_rows(ka_ref[...], 2, [ones_row(n)] * 3)], axis=0
        ).T
        values[at : at + n] = jnp.concatenate(
            [v_ref[...], put_rows(jnp.zeros((AUG, n), LOW), 0, [ones_row(n)] * 3)], axis=0
        ).T
        key_list.append(k_ref[...])
        at += n
    grads, queries = g_ref[...], q_ref[...]
    delta = jnp.sum(grads.astype(WIDE) * o_ref[...].astype(WIDE), axis=0, keepdims=True)
    query_aug = jnp.concatenate([queries, put_rows(qa_ref[...], 2, split3(-lse_ref[0]))], axis=0)
    grad_aug = jnp.concatenate([grads, put_rows(jnp.zeros((AUG, nq), LOW), 0, split3(-delta))], axis=0)
    probs = jnp.exp(dot(keys[...], query_aug, 1, 0))
    prob_grads = dot(values[...], grad_aug, 1, 0)
    low_probs = probs.astype(LOW)
    score_grads = (probs * prob_grads).astype(LOW)
    dq_ref[...] = dot(jnp.concatenate(key_list, axis=1), score_grads, 1, 0) * HEAD_DIM ** (-0.5)
    dv = dot(grads, low_probs, 1, 1)
    dk = dot(queries, score_grads, 1, 1)
    at = 0
    for dkv_ref in dkv_refs:
        n = dkv_ref.shape[2]
        dkv_ref[0] = dk[:, at : at + n].astype(dkv_ref.dtype)
        dkv_ref[1] = dv[:, at : at + n].astype(dkv_ref.dtype)
        at += n


def attend_backward(q, g, o, lse, qa, kvs, kas, types, after, first, heads):
    parts, nq = len(kvs), q.shape[1]
    sizes = [kv.shape[1] for kv in kvs]
    nk = sum(sizes)
    width = heads * HEAD_DIM
    out = pl.pallas_call(
        functools.partial(backward_kernel, parts),
        grid=(heads,),
        in_specs=[
            head_block(nq, first),
            head_block(nq, first),
            head_block(nq, 0),
            pl.BlockSpec((1, 1, nq), lambda h: (h, 0, 0)),
            whole_block(AUG, nq),
        ]
        + [head_block(n, first) for n in sizes]
        + [head_block(n, first + HEADS) for n in sizes]
        + [whole_block(AUG, n) for n in sizes]
        + [pl.BlockSpec(memory_space=pl.ANY)] * len(after),
        out_specs=[head_block(nq, 0)]
        + [pl.BlockSpec((2, HEAD_DIM, n), lambda h: (0, h, 0)) for n in sizes],
        out_shape=[jax.ShapeDtypeStruct((width, nq), WIDE)]
        + [jax.ShapeDtypeStruct((2, width, n), t) for n, t in zip(sizes, types)],
        scratch_shapes=[pltpu.VMEM((nk, HEAD_DIM + AUG), LOW)] * 2,
        compiler_params=pltpu.CompilerParams(vmem_limit_bytes=60 << 20),
        cost_estimate=cost(
            flops=30 * heads * nq * nk * HEAD_DIM,
            bytes_accessed=8 * width * (nq + nk),
            transcendentals=heads * nq * nk,
        ),
        name="attend_backward",
    )(q, g, o, lse, qa, *kvs, *kvs, *kas, *after)
    return out[0], out[1:]


def turn(values, cosine, sine):
    heads = values.reshape(-1, HEAD_DIM, values.shape[-1])
    half = HEAD_DIM // 2
    front, behind = heads[:, :half], heads[:, half:]
    turned = jnp.concatenate([front * cosine - behind * sine, behind * cosine + front * sine], axis=1)
    return turned.reshape(values.shape)


def project_kernel(kinds, w_ref, x_ref, cos_ref, sin_ref, o_ref):
    made = dot(w_ref[...], x_ref[...], 1, 1)
    for i, kind in enumerate(kinds):

        @pl.when(pl.program_id(0) == i)
        def _():
            if kind == "v":
                o_ref[...] = made.astype(LOW)
            else:
                low = turn(made, cos_ref[...], sin_ref[...]).astype(LOW)
                o_ref[...] = low * jnp.asarray(HEAD_DIM ** (-0.5), LOW) if kind == "q" else low


def project(qkv_t, x, cosine, sine, kinds, first):
    n, width = x.shape
    return pl.pallas_call(
        functools.partial(project_kernel, kinds),
        grid=(len(kinds),),
        in_specs=[
            pl.BlockSpec((width, width), lambda i: (i + first, 0)),
            pl.BlockSpec((n, width), lambda i: (0, 0)),
            whole_block(HEAD_DIM // 2, n),
            whole_block(HEAD_DIM // 2, n),
        ],
        out_specs=pl.BlockSpec((width, n), lambda i: (i, 0)),
        out_shape=jax.ShapeDtypeStruct((len(kinds) * width, n), LOW),
        compiler_params=pltpu.CompilerParams(vmem_limit_bytes=40 << 20),
        cost_estimate=cost(
            flops=2 * len(kinds) * width * width * n, bytes_accessed=6 * width * n, transcendentals=0
        ),
        name="project",
    )(qkv_t, x, cosine, sine)


def norm_forward(values, gain, shift):
    center = jnp.mean(values, axis=-1, keepdims=True)
    centered = values - center
    inverse = lax.rsqrt(jnp.mean(centered * centered, axis=-1, keepdims=True) + EPSILON)
    normed = centered * inverse
    return (normed * gain + shift, normed, inverse)


def norm_backward(grads, normed, inverse, gain):
    scaled = grads * gain
    first_mean = jnp.mean(scaled, axis=-1, keepdims=True)
    second_mean = jnp.mean(scaled * normed, axis=-1, keepdims=True)
    return inverse * (scaled - first_mean - normed * second_mean)


def middle_kernel(pieces, *refs):
    att_refs = refs[:pieces]
    x_ref, top_ref, vec_ref, out_w, gu_w, down_w = refs[pieces : pieces + 6]
    o_ref, low_ref, hid_ref, gug_ref, mix_ref, res_ref, proj_ref, att_ref, sums_ref = refs[pieces + 6 : pieces + 15]
    kept = refs[pieces + 15]
    gain_one, shift_one, gain_two, shift_two = (vec_ref[i : i + 1] for i in range(4))
    blocks, width = down_w.shape[0], down_w.shape[2]
    projected = dot(jnp.concatenate([r[...] for r in att_refs], axis=0), out_w[...], 0, 1)
    x_one, normed_one, inverse_one = norm_forward(x_ref[...].astype(WIDE) + projected, gain_one, shift_one)
    x_low = x_one.astype(LOW)
    low_ref[...] = x_low
    mixed = jnp.zeros_like(x_one)
    for j in range(blocks):
        both = dot(x_low, gu_w[j], 1, 0)
        gate, up = both[:, :width], both[:, width:]
        sigma = 0.5 * jnp.tanh(0.5 * gate) + 0.5
        activated = gate * sigma
        kept[j, :, :width] = up * (sigma + activated * (1.0 - sigma))
        kept[j, :, width:] = activated
        hidden = (activated * up).astype(LOW)
        hid_ref[j] = hidden
        mixed += dot(hidden, down_w[j], 1, 1)
    result, normed_two, inverse_two = norm_forward(x_one + mixed, gain_two, shift_two)
    o_ref[...] = result.astype(LOW)
    grad_top = top_ref[...].astype(WIDE)
    d_resid_two = norm_backward(grad_top, normed_two, inverse_two, gain_two)
    mix_grad = d_resid_two.astype(LOW)
    mix_ref[...] = mix_grad
    d_x_one = d_resid_two
    for j in range(blocks):
        hidden_grad = dot(mix_grad, down_w[j], 1, 0)
        gate_grad = (hidden_grad * kept[j, :, :width]).astype(LOW)
        up_grad = (hidden_grad * kept[j, :, width:]).astype(LOW)
        grads = jnp.concatenate([gate_grad, up_grad], axis=1)
        gug_ref[j] = grads
        d_x_one += dot(grads, gu_w[j], 1, 1)
    d_resid_one = norm_backward(d_x_one, normed_one, inverse_one, gain_one)
    res_ref[...] = d_resid_one
    proj_grad = d_resid_one.astype(LOW)
    proj_ref[...] = proj_grad
    att_ref[...] = dot(out_w[...], proj_grad, 0, 1).astype(LOW)
    sums = jnp.concatenate(
        [
            jnp.sum(v, axis=0, keepdims=True)
            for v in (d_x_one * normed_one, d_x_one, grad_top * normed_two, grad_top)
        ]
        + [jnp.zeros((4, d_x_one.shape[1]), WIDE)],
        axis=0,
    )

    @pl.when(pl.program_id(0) == 0)
    def _():
        sums_ref[...] = sums

    @pl.when(pl.program_id(0) > 0)
    def _():
        sums_ref[...] += sums


def middle(attended, x, grad_top, vectors, out_t, gu, down):
    n, width = x.shape
    blocks, _, units = down.shape
    step = min(n, 256)
    pieces = len(attended)

    def kept_block(shape):
        return pl.BlockSpec(shape, lambda i: (0,) * len(shape), pipeline_mode=pl.Buffered(1))

    rows = pl.BlockSpec((step, width), lambda i: (i, 0))
    return pl.pallas_call(
        functools.partial(middle_kernel, pieces),
        grid=(n // step,),
        in_specs=[pl.BlockSpec((a.shape[0], step), lambda i: (0, i)) for a in attended]
        + [rows, rows]
        + [kept_block(a.shape) for a in (vectors, out_t, gu, down)],
        out_specs=[
            rows,
            rows,
            pl.BlockSpec((blocks, step, units), lambda i: (0, i, 0)),
            pl.BlockSpec((blocks, step, 2 * units), lambda i: (0, i, 0)),
            rows,
            rows,
            rows,
            pl.BlockSpec((width, step), lambda i: (0, i)),
            pl.BlockSpec((8, width), lambda i: (0, 0)),
        ],
        out_shape=[
            jax.ShapeDtypeStruct((n, width), LOW),
            jax.ShapeDtypeStruct((n, width), LOW),
            jax.ShapeDtypeStruct((blocks, n, units), LOW),
            jax.ShapeDtypeStruct((blocks, n, 2 * units), LOW),
            jax.ShapeDtypeStruct((n, width), LOW),
            jax.ShapeDtypeStruct((n, width), WIDE),
            jax.ShapeDtypeStruct((n, width), LOW),
            jax.ShapeDtypeStruct((width, n), LOW),
            jax.ShapeDtypeStruct((8, width), WIDE),
        ],
        scratch_shapes=[pltpu.VMEM((blocks, step, 2 * units), WIDE)],
        compiler_params=pltpu.CompilerParams(vmem_limit_bytes=60 << 20),
        cost_estimate=cost(
            flops=2 * n * width * (2 * width + 6 * blocks * units), bytes_accessed=60 << 20, transcendentals=n * blocks * units
        ),
        name="middle",
    )(*attended, x, grad_top, vectors, out_t, gu, down)


def unturn_kernel(add, *refs):
    dq_ref, own_ref = refs[:2]
    cos_ref, sin_ref, x_ref, grad_ref, g_ref = refs[-5:]
    kind = pl.program_id(0)
    cosine, sine = cos_ref[...], -sin_ref[...]

    def emit(made):
        low = made.astype(LOW)
        grad_ref[0] = low
        g_ref[0] = dot(low, x_ref[...], 1, 0).astype(LOW)

    @pl.when(kind == 0)
    def _():
        emit(turn(dq_ref[...], cosine, sine))

    def total():
        return own_ref[0] + refs[2][0].astype(WIDE) if add else own_ref[0]

    @pl.when(kind == 1)
    def _():
        emit(turn(total(), cosine, sine))

    @pl.when(kind == 2)
    def _():
        emit(total())


def unturn(dq, own, others, cosine, sine, x):
    n, width = x.shape
    count = dq.shape[0]
    pair = pl.BlockSpec((1, count, n), lambda i: (jnp.maximum(i - 1, 0), 0, 0))
    table = whole_block(HEAD_DIM // 2, n)
    return pl.pallas_call(
        functools.partial(unturn_kernel, len(others)),
        grid=(3,),
        in_specs=[whole_block(count, n), pair] + [pair] * len(others) + [table, table, whole_block(n, width)],
        out_specs=[
            pl.BlockSpec((1, count, n), lambda i: (i, 0, 0)),
            pl.BlockSpec((1, count, width), lambda i: (i, 0, 0)),
        ],
        out_shape=[
            jax.ShapeDtypeStruct((3, count, n), LOW),
            jax.ShapeDtypeStruct((3, count, width), LOW),
        ],
        compiler_params=pltpu.CompilerParams(vmem_limit_bytes=30 << 20),
        cost_estimate=cost(flops=6 * n * width * count, bytes_accessed=9 << 20, transcendentals=0),
        name="unturn",
    )(dq, own, *others, cosine, sine, x)


def finish_kernel(groups, *refs):
    res_ref, w_ref = refs[groups : groups + 2]
    in_ref = refs[-1]
    grad = jnp.concatenate([r[kind] for kind in range(3) for r in refs[:groups]], axis=0)
    in_ref[...] = (res_ref[...] + dot(grad, w_ref[...], 0, 0)).astype(LOW)


def finish(grads, resid, qkv_t, after, part, n):
    width = resid.shape[1]
    step = min(n, 256)
    first = part * (n // step)
    rows = pl.BlockSpec((step, width), lambda i: (i + first, 0))
    return pl.pallas_call(
        functools.partial(finish_kernel, len(grads)),
        grid=(n // step,),
        in_specs=[pl.BlockSpec((3, a.shape[1], step), lambda i: (0, 0, i + first)) for a in grads]
        + [rows, pl.BlockSpec(qkv_t.shape, lambda i: (0, 0), pipeline_mode=pl.Buffered(1))]
        + [pl.BlockSpec(memory_space=pl.ANY)] * len(after),
        out_specs=pl.BlockSpec((step, width), lambda i: (i, 0)),
        out_shape=jax.ShapeDtypeStruct((n, width), LOW),
        compiler_params=pltpu.CompilerParams(vmem_limit_bytes=50 << 20),
        cost_estimate=cost(flops=6 * n * width * width, bytes_accessed=12 << 20, transcendentals=0),
        name="finish",
    )(*grads, resid, qkv_t, *after)


def beside_kernel(count, *refs):
    out = refs[-1]
    at = 0
    for ref in refs[:count]:
        n = ref.shape[1]
        out[:, at : at + n] = ref[...]
        at += n


def beside(arrays, after):
    whole = pl.BlockSpec(memory_space=pltpu.VMEM)
    total = sum(a.shape[1] for a in arrays)
    return pl.pallas_call(
        functools.partial(beside_kernel, len(arrays)),
        in_specs=[whole] * len(arrays) + [pl.BlockSpec(memory_space=pl.ANY)] * len(after),
        out_specs=whole,
        out_shape=jax.ShapeDtypeStruct((arrays[0].shape[0], total), arrays[0].dtype),
        name="beside",
    )(*arrays, *after)


def select_kernel(at, x_ref, *refs):
    outs = refs[-x_ref.shape[0] :]
    for k, out in enumerate(outs):
        out[...] = x_ref[at[k]]


def select(x, at, after):
    count = x.shape[0]
    whole = pl.BlockSpec(memory_space=pltpu.VMEM)
    return pl.pallas_call(
        select_kernel,
        in_specs=[pl.BlockSpec(memory_space=pltpu.SMEM), whole] + [pl.BlockSpec(memory_space=pl.ANY)] * len(after),
        out_specs=[whole] * count,
        out_shape=[jax.ShapeDtypeStruct(x.shape[1:], x.dtype)] * count,
        compiler_params=pltpu.CompilerParams(vmem_limit_bytes=10 << 20),
        cost_estimate=cost(flops=0, bytes_accessed=4 * x.size, transcendentals=0),
        name="select",
    )(at, x, *after)


def stack_kernel(count, *refs):
    out = refs[-1]
    at = 0
    for ref in refs[:count]:
        n = ref.shape[0]
        out[at : at + n] = ref[...]
        at += n


def stack(arrays, after=()):
    one = arrays[0]
    total = sum(a.shape[0] for a in arrays)
    whole = pl.BlockSpec(memory_space=pltpu.VMEM)
    return pl.pallas_call(
        functools.partial(stack_kernel, len(arrays)),
        in_specs=[whole] * len(arrays) + [pl.BlockSpec(memory_space=pl.ANY)] * len(after),
        out_specs=whole,
        out_shape=jax.ShapeDtypeStruct((total,) + one.shape[1:], one.dtype),
        compiler_params=pltpu.CompilerParams(vmem_limit_bytes=16 << 20),
        cost_estimate=cost(bytes_accessed=4 * one.size * len(arrays)),
        name="stack",
    )(*arrays, *after)


def arrange_kernel(cuts, place, mine, theirs, *refs):
    near, depth = mine.shape[:2]
    for half, src in enumerate((mine, theirs)):
        for r in range(near):
            spot = place[half * near + r]
            for k in range(depth):
                z = place[2 * near + k]
                for out, (start, size, z_first) in zip(refs[-len(cuts) :], cuts):
                    block = src[r, k, start : start + size]
                    if z_first:
                        out[z, spot] = block
                    else:
                        out[spot, z] = block


def arrange(mine, theirs, place, cuts, after):
    near, depth, _, width = mine.shape
    whole = pl.BlockSpec(memory_space=pltpu.VMEM)
    lead = {True: (depth, 2 * near), False: (2 * near, depth)}
    return pl.pallas_call(
        functools.partial(arrange_kernel, cuts),
        in_specs=[pl.BlockSpec(memory_space=pltpu.SMEM), whole, whole]
        + [pl.BlockSpec(memory_space=pl.ANY)] * len(after),
        out_specs=[whole] * len(cuts),
        out_shape=[
            jax.ShapeDtypeStruct(lead[z_first] + (size, width), mine.dtype) for _, size, z_first in cuts
        ],
        compiler_params=pltpu.CompilerParams(vmem_limit_bytes=30 << 20),
        cost_estimate=cost(flops=0, bytes_accessed=8 * mine.size, transcendentals=0),
        name="arrange",
    )(place, mine, theirs, *after)


def add_low(a, b):
    return (a.astype(WIDE) + b.astype(WIDE)).astype(LOW)


def join_core_kernel(axis, place, mine, got, *refs):
    outs = refs[-2:]
    for i in range(4):
        for t in range(mine.shape[1 - axis]):
            spot = (place[i], t) if axis == 0 else (t, place[i])
            outs[i // 2][i % 2, t] = add_low(mine[spot], got[spot])


def join_far_kernel(keep, got, *refs):
    for i, out in enumerate(refs[-2:]):
        out[...] = add_low(keep[i], got[i])


def join_near_kernel(place, keep, got, *refs):
    for k, out in enumerate(refs[-keep.shape[0] :]):
        out[...] = add_low(keep[place[k]], got[place[k]])


def join(kernel, arrays, shapes, after, scalars=()):
    whole = pl.BlockSpec(memory_space=pltpu.VMEM)
    return pl.pallas_call(
        kernel,
        in_specs=[pl.BlockSpec(memory_space=pltpu.SMEM)] * len(scalars)
        + [whole] * len(arrays)
        + [pl.BlockSpec(memory_space=pl.ANY)] * len(after),
        out_specs=[whole] * len(shapes),
        out_shape=[jax.ShapeDtypeStruct(shape, LOW) for shape in shapes],
        compiler_params=pltpu.CompilerParams(vmem_limit_bytes=24 << 20),
        cost_estimate=cost(bytes_accessed=8 * arrays[0].size),
        name="join",
    )(*scalars, *arrays, *after)


def side_kernel(pieces, core_ref, mix_ref, hid_ref, proj_ref, *refs):
    att_refs = refs[:pieces]
    norm_ref, mine, send, turned, result, side = refs[pieces:]
    j = pl.program_id(0)
    lines, count = mine.shape[2], mix_ref.shape[1] // (2 * mine.shape[1])
    extra = norm_ref.shape[2]
    few = lines - count - extra

    @pl.when(j == 0)
    def _():
        turned[...] = mix_ref[...].T
        side[...] = dot(proj_ref[...].T, jnp.concatenate([r[...] for r in att_refs], axis=0), 1, 1)

    result[...] = dot(turned[...], hid_ref[0], 1, 0)
    for p in range(mine.shape[1]):
        for rel, out in enumerate((mine, send)):
            dp = 2 * p + (core_ref[0] + rel) % 2
            rows = result[pl.ds(pl.multiple_of(dp * count, 8), count)]
            small = side[pl.ds(pl.multiple_of((dp * pl.num_programs(0) + j) * few, 8), few)]
            out[0, p, :count] = rows.astype(LOW)
            out[0, p, count:] = jnp.concatenate([small, norm_ref[dp, 0]], axis=0).astype(LOW)


def side_grads(core, mix_grad, hidden, proj_grad, attended, norms, lines):
    n, width = mix_grad.shape
    blocks, chips = hidden.shape[0], norms.shape[0] // 2
    whole = pl.BlockSpec((n, width), lambda j: (0, 0))
    out = pl.BlockSpec((1, chips, lines, width), lambda j: (j, 0, 0, 0))
    return pl.pallas_call(
        functools.partial(side_kernel, len(attended)),
        grid=(blocks,),
        in_specs=[
            pl.BlockSpec(memory_space=pltpu.SMEM),
            whole,
            pl.BlockSpec((1, n, width), lambda j: (j, 0, 0)),
            whole,
        ]
        + [whole_block(*a.shape) for a in attended]
        + [pl.BlockSpec((2 * chips, 1, norms.shape[2], width), lambda j: (0, j, 0, 0))],
        out_specs=[out] * 2,
        out_shape=[jax.ShapeDtypeStruct((blocks, chips, lines, width), LOW)] * 2,
        scratch_shapes=[
            pltpu.VMEM((width, n), LOW),
            pltpu.VMEM((width, width), WIDE),
            pltpu.VMEM((width, width), WIDE),
        ],
        compiler_params=pltpu.CompilerParams(vmem_limit_bytes=40 << 20),
        cost_estimate=cost(flops=10 * n * width * width, bytes_accessed=16 << 20),
        name="side_grads",
    )(core.reshape(1), mix_grad, hidden, proj_grad, *attended, norms)


def gate_up_kernel(x_ref, g_ref, *refs):
    out, turned = refs[-2:]

    @pl.when(pl.program_id(0) == 0)
    def _():
        turned[...] = x_ref[...].T

    out[0] = dot(turned[...], g_ref[0], 1, 0).astype(LOW)


def gate_up_grads(x, grads, after):
    n, width = x.shape
    blocks, _, both = grads.shape
    return pl.pallas_call(
        gate_up_kernel,
        grid=(blocks,),
        in_specs=[pl.BlockSpec((n, width), lambda j: (0, 0)), pl.BlockSpec((1, n, both), lambda j: (j, 0, 0))]
        + [pl.BlockSpec(memory_space=pl.ANY)] * len(after),
        out_specs=pl.BlockSpec((1, width, both), lambda j: (j, 0, 0)),
        out_shape=jax.ShapeDtypeStruct((blocks, width, both), LOW),
        scratch_shapes=[pltpu.VMEM((width, n), LOW)],
        compiler_params=pltpu.CompilerParams(vmem_limit_bytes=40 << 20),
        cost_estimate=cost(flops=2 * n * width * blocks * both, bytes_accessed=24 << 20, scale=1),
        name="gate_up_grads",
    )(x, grads, *after)


def local(
    tp, ways, tokens, segment_ids, positions, w_qkv, w_out, norm1_gain, norm1_shift, w_gate, w_up, w_down, norm2_gain, norm2_shift, out_grad
):
    rows, piece, width = tokens.shape
    chips, per_group = ways
    dp, near = 2 * chips, tp // per_group
    line = ("core", "zg", "zm")
    flat = ("zg", "zm")
    everyone = ("zg", "zm", "chip", "core")
    core = lax.axis_index("core")
    chip = lax.axis_index("chip")
    group = lax.axis_index("zg")
    z = group * near + lax.axis_index("zm")
    member = lax.axis_index("zm") * 2 + core
    own = rows * piece
    by_hand = chips == 4 and tp == 4

    def ring(step):
        pairs = []
        for c in range(2):
            for j in range(tp):
                row = c * rows + (j + step) % rows
                m = j // rows
                pairs.append((c * tp + j, (m % 2) * tp + row * near + m // 2))
        return pairs

    def bring(x, after=()):
        at = jnp.stack([(z + k) % rows for k in range(rows)]).astype(jnp.int32)
        return [lax.ppermute(a, line, ring(k)) for k, a in enumerate(select(x, at, after))]

    def give_back(parts):
        back = [lax.ppermute(part, line, [(b, a) for a, b in ring(k)]) for k, part in enumerate(parts)]
        return jnp.roll(jnp.stack(back), z, axis=0)

    def hop(x, first):
        pairs = []
        for p in range(4):
            for c in range(2):
                bit = 1 if (c == 0) == first else 2
                pairs.append((p * 2 + c, (p ^ bit) * 2 + c))
        return lax.ppermute(x, ("chip", "core"), pairs)

    def along(x, k):
        return lax.ppermute(x, flat, [(i, (i + k) % tp) for i in range(tp)])

    mask_one, mask_two = jnp.where(core == 0, 1, 2), jnp.where(core == 0, 2, 1)

    def spread_z(x, after=()):
        return stack([x[None]] + [along(x, k)[None] for k in range(1, tp)], after) if by_hand else x

    def spread_near(column, after=()):
        return stack([column, hop(column, True)], after) if by_hand else column

    def spread_far(pair, after=()):
        return stack([pair, hop(pair, False)], after) if by_hand else pair

    def spread_core(mine, cuts, after=()):
        if not by_hand:
            whole = lax.all_gather(mine, everyone, axis=0, tiled=False).reshape((tp, dp) + mine.shape)
            parts = [(whole[:, :, at : at + size], z_first) for at, size, z_first in cuts]
            return [a if z_first else a.swapaxes(0, 1) for a, z_first in parts]
        theirs = lax.ppermute(mine, "core", SWAP)
        place = [(chip ^ m) * 2 + core for m in (0, mask_one, mask_two, 3)]
        place += [(chip ^ m) * 2 + 1 - core for m in (0, mask_two, mask_one, 3)]
        place += [(z - k) % tp for k in range(tp)]
        mine, theirs = (a.reshape((chips, tp) + a.shape[1:]) for a in (mine, theirs))
        return arrange(mine, theirs, jnp.stack(place).astype(jnp.int32), cuts, after)

    pick = lambda a, i, axis: lax.dynamic_index_in_dim(a, i, axis, False)
    near_place = jnp.stack([chip, chip ^ mask_one, chip ^ mask_two, chip ^ 3]).astype(jnp.int32)
    line_place = jnp.stack([(z + k) % tp for k in range(tp)]).astype(jnp.int32)

    def collapse_core(mine, send, axis, after=()):
        got = lax.ppermute(send, "core", SWAP)
        shape = (2,) + mine.shape[: axis] + mine.shape[axis + 1 :]
        return join(functools.partial(join_core_kernel, axis), [mine, got], [shape] * 2, after, (near_place,))

    def collapse_far(keep, send, after=()):
        return join(join_far_kernel, [keep, hop(send, False)], [keep.shape[1:]] * 2, after)

    def collapse_near(keep, send, after=()):
        return join(join_near_kernel, [keep, hop(send, True)], [keep.shape[1:]] * tp, after, (line_place,))

    def collapse_z(parts):
        total = parts[0].astype(WIDE)
        for k in range(1, tp):
            total += along(parts[k], k).astype(WIDE)
        return total

    def collapse_all(x):
        return lax.psum_scatter(
            x.reshape((tp * dp,) + x.shape[2:]), everyone, scatter_dimension=0, tiled=False
        ).astype(WIDE)

    nq, no = w_qkv.shape[1], w_out.shape[1]
    units = w_gate.shape[1]
    blocks = tp * units // width
    merged = by_hand and units == width
    pad = -(no + 1) % 16
    norm_row = jnp.concatenate([norm1_gain, norm1_shift, norm2_gain, norm2_shift])
    norm_row = jnp.pad(norm_row, (0, width - 4 * no))[None]
    small = jnp.concatenate([w_out.T, norm_row, jnp.zeros((pad, width), LOW)])
    brought = bring(tokens)
    x = jnp.concatenate(brought)
    qkv_t = spread_near(spread_z(w_qkv.T, tuple(brought)))
    qkv_t = spread_far(qkv_t)
    qkv_t = spread_core(qkv_t, [(0, nq, False)])[0].reshape(3 * width, width)
    gu = beside([w_gate, w_up], tuple(brought))
    gu = lax.all_gather(gu, everyone, axis=0, tiled=False)
    gu = gu.reshape(blocks, tp // blocks, width, 2, units).transpose(0, 2, 3, 1, 4).reshape(blocks, width, -1)

    info = jnp.stack([segment_ids, positions])
    other = lax.ppermute(info, "core", SWAP)
    info = jnp.where(core == 0, jnp.stack([info, other], 1), jnp.stack([other, info], 1))
    info = info.reshape(2, 2 * rows, -1)
    info = lax.dynamic_index_in_dim(info, group, 1, False)
    second = (info[0] != info[0, 0]).reshape(-1, rows, piece)
    second = jnp.roll(second[:, ::-1], group + 1, axis=1).reshape(-1, own)
    places = info[1].reshape(-1, rows, piece)
    places = jnp.roll(places[:, ::-1], group + 1, axis=1).reshape(-1, own)
    own_second = lax.dynamic_index_in_dim(second, member, 0, False)
    own_places = lax.dynamic_index_in_dim(places, member, 0, False)

    def key_aug(is_second):
        return jnp.pad(
            jnp.stack([jnp.where(is_second, 0.0, -MASK), jnp.where(is_second, -MASK, 0.0)]), ((0, AUG - 2), (0, 0))
        ).astype(LOW)

    query_aug = jnp.pad(
        jnp.stack([own_second, ~own_second]).astype(WIDE), ((0, AUG - 2), (0, 0))
    ).astype(LOW)

    half = HEAD_DIM // 2
    frequency = 1000.0 ** (-(jnp.arange(half, dtype=WIDE) * 2.0) / HEAD_DIM)
    angles = own_places.astype(WIDE)[None] * frequency[:, None]
    cosine, sine = jnp.cos(angles), jnp.sin(angles)

    kv = project(qkv_t, x, cosine, sine, "kv", 1)
    members = 2 * near
    if members == 2:
        kvs = [kv, lax.ppermute(kv, "core", SWAP)]
        other_second = lax.dynamic_index_in_dim(second, 1 - member, 0, False)
        kas = [key_aug(own_second), key_aug(other_second)]
        types = [WIDE, LOW]
    else:
        kvs = [lax.all_gather(kv, ("zm", "core"), axis=1, tiled=True)]
        kas = [key_aug(second.reshape(-1))]
        types = [LOW]
    q = project(qkv_t, x, cosine, sine, "q", 0)
    spans = [(i * HEADS // PIECES, HEADS // PIECES) for i in range(PIECES)]
    late = stack([w_down.T, small] if merged else [small], (x,))
    attended, lses = [], []
    cuts = [(0, width // dp, True), (width // dp, small.shape[0], False)]
    for i, span in enumerate(spans):
        att, lse = attend_forward(q, query_aug, kvs, kas, (late,) if i else (), *span)
        attended.append(att)
        lses.append(lse)
        if i == 0:
            late = spread_z(late, (att,))
            top_parts = bring(out_grad, (att, late))
        if i == 1:
            late = spread_near(late, (att,))
        if i == 2:
            late = spread_far(late, (att,))
    late = spread_core(late, cuts if merged else [(0, small.shape[0], False)])
    grad_top = stack(top_parts, (attended[-1],))
    by_column = late[-1]
    down = late[0] if merged else spread_core(w_down.T, [(0, width // dp, True)])[0]
    down = down.reshape(blocks, tp // blocks, width, units).swapaxes(1, 2).reshape(blocks, width, -1)
    out_t = by_column[:, :, :no].reshape(width, width)
    vectors = by_column[:, :, no, : 4 * no].reshape(dp * tp, 4, no).swapaxes(0, 1).reshape(4, width)
    vectors = jnp.pad(vectors.astype(WIDE), ((0, 4), (0, 0)))

    output, x_low, hidden, gug, mix_grad, d_resid_one, proj_grad, att_grad, sums = middle(
        attended, x, grad_top, vectors, out_t, gu, down
    )
    output = give_back([output[k * piece : (k + 1) * piece] for k in range(rows)])

    def ungroup(g, parts):
        g = g.reshape(blocks, width, parts, tp // blocks, units).transpose(0, 3, 1, 2, 4)
        return g.reshape(tp, dp, width // dp, parts * units)

    norms = sums[:4].reshape(4, dp * tp, no).swapaxes(0, 1).reshape(dp, tp, 1, 4 * no)
    if merged:
        norms = jnp.pad(norms, ((0, 0), (0, 0), (0, pad), (0, width - 4 * no)))
        mine, send = side_grads(core, mix_grad, hidden, proj_grad, attended, norms, width // dp + no + pad + 1)
    else:
        norms = jnp.pad(norms.astype(LOW), ((0, 0), (0, 0), (0, pad), (0, width - 4 * no)))
        g_out = dot(proj_grad, jnp.concatenate(attended), 0, 1).astype(LOW)
        side = jnp.concatenate([g_out.reshape(dp, tp, no, width), norms], axis=2)
        side = collapse_all(side.swapaxes(0, 1))
        g_down = jnp.einsum("td,jtf->jdf", mix_grad, hidden, preferred_element_type=WIDE).astype(LOW)
        g_down = collapse_all(ungroup(g_down, 1))
        mine = mix_grad
    g_gu = ungroup(gate_up_grads(x_low, gug, (mine,)), 2)
    shared_gu = collapse_all(g_gu)
    held = (g_gu,)
    if merged:
        held = collapse_core(mine, send, 1, (g_gu,))

    grads, parts = [], []
    for i, ((start, count), att, lse) in enumerate(zip(spans, attended, lses)):
        after = tuple(held) + ((output,) if i + 1 == PIECES else ())
        dq, dkv = attend_backward(q, att_grad, att, lse, query_aug, kvs, kas, types, after, start, count)
        if merged and i == 0:
            held = collapse_far(*held, (dq,))
        if merged and i == 2:
            held = collapse_near(*held, (dq,))
        if members == 2:
            own_dkv, others = dkv[0], (lax.ppermute(dkv[1], "core", SWAP),)
        else:
            summed = lax.psum_scatter(dkv[0], ("zm", "core"), scatter_dimension=2, tiled=True)
            own_dkv, others = summed.astype(WIDE), ()
        grad, part = unturn(dq, own_dkv, others, cosine, sine, x)
        grads.append(grad)
        parts.append(part)
    if merged:
        total = collapse_z(held)
        g_down, side = total[: width // dp], total[width // dp :]
    g_qkv = jnp.concatenate(parts, axis=1).reshape(dp, tp, nq, width)
    if not by_hand:
        g_qkv = collapse_all(g_qkv.swapaxes(0, 1))
        in_grad = finish(grads, d_resid_one, qkv_t, (), 0, own)
        in_grad = give_back([in_grad[k * piece : (k + 1) * piece] for k in range(rows)])
    else:
        g_qkv = g_qkv.reshape(chips, 2, tp, nq, width)
        mine, send = pick(g_qkv, core, 1), pick(g_qkv, 1 - core, 1)
        in_grad = [finish(grads, d_resid_one, qkv_t, (send,) + ((total,) if merged else ()), 0, piece)]
        held = collapse_core(mine, send, 0, (in_grad[0],))
        for k in range(1, rows):
            in_grad.append(finish(grads, d_resid_one, qkv_t, (held[0],), k, piece))
        held = collapse_far(*held, (in_grad[-1],))
        g_qkv = collapse_z(collapse_near(*held))
        in_grad = give_back(in_grad)
    vector_grads = side[no, : 4 * no].reshape(4, no)
    return (
        output,
        in_grad,
        g_qkv.T,
        side[:no].T,
        vector_grads[0],
        vector_grads[1],
        shared_gu[:, :units],
        shared_gu[:, units:],
        g_down.T,
        vector_grads[2],
        vector_grads[3],
    )


def solution(mesh):
    dp, tp = mesh.shape["dp"], mesh.shape["tp"]

    def run(*arrays):
        rows = arrays[0].shape[0] // dp
        groups = 2 * rows
        grid = Mesh(
            mesh.devices.reshape(dp // 2, 2, groups, tp // groups), ("chip", "core", "zg", "zm")
        )
        d, t = ("chip", "core"), ("zg", "zm")
        both = d + t
        placed = (
            P(d, t, None),
            P(d, None),
            P(d, None),
            P(None, both),
            P(None, both),
            P(both),
            P(both),
            P(d, t),
            P(d, t),
            P(t, d),
            P(both),
            P(both),
            P(d, t, None),
        )
        return jax.shard_map(
            functools.partial(local, tp, (dp // 2, groups)),
            mesh=grid,
            in_specs=placed,
            out_specs=(
                P(d, t, None),
                P(d, t, None),
                P(None, both),
                P(None, both),
                P(both),
                P(both),
                P(d, t),
                P(d, t),
                P(t, d),
                P(both),
                P(both),
            ),
            check_vma=False,
        )(*arrays)

    return run
```

```python
import functools

import jax
import jax.numpy as jnp
from jax import lax
from jax.experimental import pallas as pl
from jax.experimental.pallas import tpu as pltpu
import numpy as np
from jax.sharding import Mesh, PartitionSpec as P

HEADS = 12
HEAD_DIM = 64
EPSILON = 1e-05
AUG = 16
PIECES = 4
COST = 16
CHUNK = 512
MASK = 2.0**99
LOW = jnp.bfloat16
WIDE = jnp.float32
SWAP = [(0, 1), (1, 0)]


def dot(a, b, ca, cb):
    return lax.dot_general(a, b, (((ca,), (cb,)), ((), ())), preferred_element_type=WIDE)


def cost(flops=0, bytes_accessed=0, transcendentals=0, scale=COST):
    return pl.CostEstimate(
        flops=flops // scale, bytes_accessed=bytes_accessed // scale, transcendentals=transcendentals // scale
    )


def far(*arrays):
    return [pltpu.with_memory_space_constraint(a, pltpu.HBM) for a in arrays]


def split3(x):
    high = x.astype(LOW)
    rest = x - high.astype(WIDE)
    middle = rest.astype(LOW)
    return [high, middle, (rest - middle.astype(WIDE)).astype(LOW)]


def put_rows(base, at, rows):
    index = lax.broadcasted_iota(jnp.int32, base.shape, 0)
    out = base.astype(WIDE)
    for i, row in enumerate(rows):
        out = jnp.where(index == at + i, row.astype(WIDE), out)
    return out.astype(LOW)


def ones_row(n):
    return jnp.ones((1, n), WIDE)


def forward_kernel(parts, *refs):
    q_ref, qa_ref = refs[:2]
    refs = refs[: 2 + 3 * parts] + refs[-3:]
    k_refs, v_refs, ka_refs = refs[2 : 2 + parts], refs[2 + parts : 2 + 2 * parts], refs[2 + 2 * parts : 2 + 3 * parts]
    o_ref, lse_ref, keys = refs[2 + 3 * parts :]
    at = 0
    values = []
    for k_ref, v_ref, ka_ref in zip(k_refs, v_refs, ka_refs):
        n = k_ref.shape[1]
        keys[at : at + n] = jnp.concatenate([k_ref[...], ka_ref[...]], axis=0).T
        values.append(v_ref[...])
        at += n
    queries = jnp.concatenate([q_ref[...], qa_ref[...]], axis=0)
    scores = dot(keys[...], queries, 1, 0)
    top = jnp.max(scores, axis=0, keepdims=True)
    terms = jnp.exp(scores - top)
    total = jnp.sum(terms, axis=0, keepdims=True)
    result = dot(jnp.concatenate(values, axis=1), terms.astype(LOW), 1, 0)
    o_ref[...] = (result / total).astype(LOW)
    lse_ref[...] = (top + jnp.log(total)).reshape(1, 1, -1)


def head_block(n, first):
    return pl.BlockSpec((HEAD_DIM, n), lambda h: (h + first, 0))


def whole_block(rows, n):
    return pl.BlockSpec((rows, n), lambda h: (0, 0))


def attend_forward(q, qa, kvs, kas, after, first, heads):
    parts, nq = len(kvs), q.shape[1]
    sizes = [kv.shape[1] for kv in kvs]
    nk = sum(sizes)
    return pl.pallas_call(
        functools.partial(forward_kernel, parts),
        grid=(heads,),
        in_specs=[head_block(nq, first), whole_block(AUG, nq)]
        + [head_block(n, first) for n in sizes]
        + [head_block(n, first + HEADS) for n in sizes]
        + [whole_block(AUG, n) for n in sizes]
        + [pl.BlockSpec(memory_space=pl.ANY)] * len(after),
        out_specs=[head_block(nq, 0), pl.BlockSpec((1, 1, nq), lambda h: (h, 0, 0))],
        out_shape=[
            jax.ShapeDtypeStruct((heads * HEAD_DIM, nq), LOW),
            jax.ShapeDtypeStruct((heads, 1, nq), WIDE),
        ],
        scratch_shapes=[pltpu.VMEM((nk, HEAD_DIM + AUG), LOW)],
        compiler_params=pltpu.CompilerParams(vmem_limit_bytes=28 << 20),
        cost_estimate=cost(
            flops=16 * heads * nq * nk * HEAD_DIM,
            bytes_accessed=4 * heads * HEAD_DIM * (nq + nk),
            transcendentals=heads * nq * nk,
        ),
        name="attend_forward",
    )(*far(q), qa, *far(*kvs), *far(*kvs), *kas, *after)


def backward_kernel(parts, *refs):
    q_ref, g_ref, o_ref, lse_ref, qa_ref = refs[:5]
    refs = refs[: 5 + 3 * parts] + refs[-3 - parts :]
    k_refs, v_refs, ka_refs = refs[5 : 5 + parts], refs[5 + parts : 5 + 2 * parts], refs[5 + 2 * parts : 5 + 3 * parts]
    dq_ref = refs[5 + 3 * parts]
    dkv_refs = refs[6 + 3 * parts : 6 + 4 * parts]
    keys, values = refs[6 + 4 * parts :]
    nq = q_ref.shape[1]
    at = 0
    for k_ref, v_ref, ka_ref in zip(k_refs, v_refs, ka_refs):
        n = k_ref.shape[1]
        keys[at : at + n] = jnp.concatenate(
            [k_ref[...], put_rows(ka_ref[...], 2, [ones_row(n)] * 3)], axis=0
        ).T
        values[at : at + n] = jnp.concatenate(
            [v_ref[...], put_rows(jnp.zeros((AUG, n), LOW), 0, [ones_row(n)] * 3)], axis=0
        ).T
        at += n
    grads, queries = g_ref[...], q_ref[...]
    delta = jnp.sum(grads.astype(WIDE) * o_ref[...].astype(WIDE), axis=0, keepdims=True)
    query_aug = jnp.concatenate([queries, put_rows(qa_ref[...], 2, split3(-lse_ref[0]))], axis=0)
    grad_aug = jnp.concatenate([grads, put_rows(jnp.zeros((AUG, nq), LOW), 0, split3(-delta))], axis=0)
    at = 0
    dq = jnp.zeros((HEAD_DIM, nq), WIDE)
    for k_ref, dkv_ref in zip(k_refs, dkv_refs):
        n = k_ref.shape[1]
        step = min(n, CHUNK)
        for start in range(0, n, step):
            lines = slice(at, at + step)
            spot = slice(start, start + step)
            probs = jnp.exp(dot(keys[lines], query_aug, 1, 0))
            prob_grads = dot(values[lines], grad_aug, 1, 0)
            score_grads = (probs * prob_grads).astype(LOW)
            dq += dot(k_ref[:, spot], score_grads, 1, 0)
            dkv_ref[0, :, spot] = dot(score_grads, queries, 1, 1).T.astype(dkv_ref.dtype)
            dkv_ref[1, :, spot] = dot(probs.astype(LOW), grads, 1, 1).T.astype(dkv_ref.dtype)
            at += step
    dq_ref[...] = dq * HEAD_DIM ** (-0.5)


def attend_backward(q, g, o, lse, qa, kvs, kas, types, after, first, heads):
    parts, nq = len(kvs), q.shape[1]
    sizes = [kv.shape[1] for kv in kvs]
    nk = sum(sizes)
    width = heads * HEAD_DIM
    out = pl.pallas_call(
        functools.partial(backward_kernel, parts),
        grid=(heads,),
        in_specs=[
            head_block(nq, first),
            head_block(nq, first),
            head_block(nq, first),
            pl.BlockSpec((1, 1, nq), lambda h: (h + first, 0, 0)),
            whole_block(AUG, nq),
        ]
        + [head_block(n, first) for n in sizes]
        + [head_block(n, first + HEADS) for n in sizes]
        + [whole_block(AUG, n) for n in sizes]
        + [pl.BlockSpec(memory_space=pl.ANY)] * len(after),
        out_specs=[head_block(nq, 0)]
        + [pl.BlockSpec((2, HEAD_DIM, n), lambda h: (0, h, 0)) for n in sizes],
        out_shape=[jax.ShapeDtypeStruct((width, nq), WIDE)]
        + [jax.ShapeDtypeStruct((2, width, n), t) for n, t in zip(sizes, types)],
        scratch_shapes=[pltpu.VMEM((nk, HEAD_DIM + AUG), LOW)] * 2,
        compiler_params=pltpu.CompilerParams(vmem_limit_bytes=24 << 20),
        cost_estimate=cost(
            flops=30 * heads * nq * nk * HEAD_DIM,
            bytes_accessed=8 * width * (nq + nk),
            transcendentals=heads * nq * nk,
        ),
        name="attend_backward",
    )(*far(q, g, o), lse, qa, *far(*kvs), *far(*kvs), *kas, *after)
    return out[0], out[1:]


def turn(values, cosine, sine):
    heads = values.reshape(-1, HEAD_DIM, values.shape[-1])
    half = HEAD_DIM // 2
    front, behind = heads[:, :half], heads[:, half:]
    turned = jnp.concatenate([front * cosine - behind * sine, behind * cosine + front * sine], axis=1)
    return turned.reshape(values.shape)


def project_kernel(kinds, w_ref, x_ref, cos_ref, sin_ref, o_ref):
    made = dot(w_ref[...], x_ref[...], 1, 1)
    for i, kind in enumerate(kinds):

        @pl.when(pl.program_id(0) == i)
        def _():
            if kind == "v":
                o_ref[...] = made.astype(LOW)
            else:
                low = turn(made, cos_ref[...], sin_ref[...]).astype(LOW)
                o_ref[...] = low * jnp.asarray(HEAD_DIM ** (-0.5), LOW) if kind == "q" else low


def project(qkv_t, x, cosine, sine, kinds, first):
    n, width = x.shape
    return pl.pallas_call(
        functools.partial(project_kernel, kinds),
        grid=(len(kinds),),
        in_specs=[
            pl.BlockSpec((width, width), lambda i: (i + first, 0)),
            pl.BlockSpec((n, width), lambda i: (0, 0)),
            whole_block(HEAD_DIM // 2, n),
            whole_block(HEAD_DIM // 2, n),
        ],
        out_specs=pl.BlockSpec((width, n), lambda i: (i, 0)),
        out_shape=jax.ShapeDtypeStruct((len(kinds) * width, n), LOW),
        compiler_params=pltpu.CompilerParams(vmem_limit_bytes=40 << 20),
        cost_estimate=cost(
            flops=2 * len(kinds) * width * width * n, bytes_accessed=6 * width * n, transcendentals=0
        ),
        name="project",
    )(qkv_t, x, cosine, sine)


def norm_forward(values, gain, shift):
    center = jnp.mean(values, axis=-1, keepdims=True)
    centered = values - center
    inverse = lax.rsqrt(jnp.mean(centered * centered, axis=-1, keepdims=True) + EPSILON)
    normed = centered * inverse
    return (normed * gain + shift, normed, inverse)


def norm_backward(grads, normed, inverse, gain):
    scaled = grads * gain
    first_mean = jnp.mean(scaled, axis=-1, keepdims=True)
    second_mean = jnp.mean(scaled * normed, axis=-1, keepdims=True)
    return inverse * (scaled - first_mean - normed * second_mean)


def middle_kernel(parts, few, *refs):
    att_in, x_ref, top_ref, pack = refs[:4]
    low_ref, hid_ref, gug_ref, mix_ref, res_ref, proj_ref, att_ref, sums_ref = refs[-12 - parts : -4 - parts]
    o_refs, kept, wide, out_w, vec_ref = refs[-4 - parts : -4], *refs[-4:]
    blocks, width = pack.shape[0], pack.shape[3]
    lines = width // pack.shape[1]
    if few:

        @pl.when(pl.program_id(0) == 0)
        def _():
            total = jnp.zeros((8, width), WIDE)
            for j in range(blocks):
                for i in range(pack.shape[1]):
                    rows = pack[j, i, 3 * lines :].astype(WIDE)
                    spot = (i * blocks + j) * few
                    wide[spot : spot + few] = rows[:few]
                    total += rows[few : few + 8]
            out_w[...] = wide[...].astype(LOW)
            vec_ref[...] = total

    else:
        out_w, vec_ref = refs[4:6]
    gain_one, shift_one, gain_two, shift_two = (vec_ref[i : i + 1] for i in range(4))

    def weight(j, kind):
        return pack[j, :, kind * lines : (kind + 1) * lines].reshape(width, width)

    projected = dot(att_in[...], out_w[...], 0, 1)
    x_one, normed_one, inverse_one = norm_forward(x_ref[...].astype(WIDE) + projected, gain_one, shift_one)
    x_low = x_one.astype(LOW)
    low_ref[...] = x_low
    mixed = jnp.zeros_like(x_one)
    for j in range(blocks):
        gate = dot(x_low, weight(j, 0), 1, 0)
        up = dot(x_low, weight(j, 1), 1, 0)
        sigma = 0.5 * jnp.tanh(0.5 * gate) + 0.5
        activated = gate * sigma
        kept[j, :, :width] = up * (sigma + activated * (1.0 - sigma))
        kept[j, :, width:] = activated
        hidden = (activated * up).astype(LOW)
        hid_ref[j] = hidden
        mixed += dot(hidden, weight(j, 2), 1, 1)
    result, normed_two, inverse_two = norm_forward(x_one + mixed, gain_two, shift_two)
    steps = pl.num_programs(0) // parts
    for k, o_ref in enumerate(o_refs):

        @pl.when(pl.program_id(0) // steps == k)
        def _():
            o_ref[...] = result.astype(LOW)

    grad_top = top_ref[...].astype(WIDE)
    d_resid_two = norm_backward(grad_top, normed_two, inverse_two, gain_two)
    mix_grad = d_resid_two.astype(LOW)
    mix_ref[...] = mix_grad
    d_x_one = d_resid_two
    for j in range(blocks):
        hidden_grad = dot(mix_grad, weight(j, 2), 1, 0)
        gate_grad = (hidden_grad * kept[j, :, :width]).astype(LOW)
        up_grad = (hidden_grad * kept[j, :, width:]).astype(LOW)
        gug_ref[j, :, :width] = gate_grad
        gug_ref[j, :, width:] = up_grad
        d_x_one += dot(gate_grad, weight(j, 0), 1, 1) + dot(up_grad, weight(j, 1), 1, 1)
    d_resid_one = norm_backward(d_x_one, normed_one, inverse_one, gain_one)
    res_ref[...] = d_resid_one
    proj_grad = d_resid_one.astype(LOW)
    proj_ref[...] = proj_grad
    att_ref[...] = dot(out_w[...], proj_grad, 0, 1).astype(LOW)
    sums = jnp.concatenate(
        [
            jnp.sum(v, axis=0, keepdims=True)
            for v in (d_x_one * normed_one, d_x_one, grad_top * normed_two, grad_top)
        ]
        + [jnp.zeros((4, d_x_one.shape[1]), WIDE)],
        axis=0,
    )

    @pl.when(pl.program_id(0) == 0)
    def _():
        sums_ref[...] = sums

    @pl.when(pl.program_id(0) > 0)
    def _():
        sums_ref[...] += sums


def middle(attended, x, grad_top, pack, small, parts):
    n, width = x.shape
    blocks, units = pack.shape[0], width
    step = min(n // parts, 256)
    steps = n // step // parts
    few = 0 if small else width // (blocks * pack.shape[1])

    def kept_block(shape):
        return pl.BlockSpec(shape, lambda i: (0,) * len(shape), pipeline_mode=pl.Buffered(1))

    def part_block(k):
        return pl.BlockSpec((step, width), lambda i: (jnp.clip(i - k * steps, 0, steps - 1), 0))

    rows = pl.BlockSpec((step, width), lambda i: (i, 0))
    out = pl.pallas_call(
        functools.partial(middle_kernel, parts, few),
        grid=(n // step,),
        in_specs=[pl.BlockSpec((width, step), lambda i: (0, i)), rows, rows]
        + [kept_block(a.shape) for a in (pack,) + small],
        out_specs=[
            rows,
            pl.BlockSpec((blocks, step, units), lambda i: (0, i, 0)),
            pl.BlockSpec((blocks, step, 2 * units), lambda i: (0, i, 0)),
            rows,
            rows,
            rows,
            pl.BlockSpec((width, step), lambda i: (0, i)),
            pl.BlockSpec((8, width), lambda i: (0, 0)),
        ]
        + [part_block(k) for k in range(parts)],
        out_shape=[
            pltpu.HBM((n, width), LOW),
            pltpu.HBM((blocks, n, units), LOW),
            pltpu.HBM((blocks, n, 2 * units), LOW),
            pltpu.HBM((n, width), LOW),
            pltpu.HBM((n, width), WIDE),
            pltpu.HBM((n, width), LOW),
            pltpu.HBM((width, n), LOW),
            jax.ShapeDtypeStruct((8, width), WIDE),
        ]
        + [pltpu.HBM((n // parts, width), LOW)] * parts,
        scratch_shapes=[
            pltpu.VMEM((blocks, step, 2 * units), WIDE),
            pltpu.VMEM((width, width), WIDE),
            pltpu.VMEM((width, width), LOW),
            pltpu.VMEM((8, width), WIDE),
        ],
        compiler_params=pltpu.CompilerParams(vmem_limit_bytes=60 << 20),
        cost_estimate=cost(
            flops=2 * n * width * (2 * width + 6 * blocks * units), bytes_accessed=60 << 20, transcendentals=n * blocks * units
        ),
        name="middle",
    )(*far(attended, x, grad_top, pack), *small)
    return out[:8], out[8:]


def unturn_kernel(add, *refs):
    dq_ref, own_ref = refs[:2]
    cos_ref, sin_ref, x_ref = refs[2 + add : 5 + add]
    grad_ref, g_ref = refs[-2:]
    kind = pl.program_id(0)
    cosine, sine = cos_ref[...], -sin_ref[...]

    def emit(made):
        low = made.astype(LOW)
        grad_ref[0] = low
        g_ref[0] = dot(low, x_ref[...], 1, 0).astype(LOW)

    @pl.when(kind == 0)
    def _():
        emit(turn(dq_ref[...], cosine, sine))

    def total():
        return own_ref[0] + refs[2][0].astype(WIDE) if add else own_ref[0]

    @pl.when(kind == 1)
    def _():
        emit(turn(total(), cosine, sine))

    @pl.when(kind == 2)
    def _():
        emit(total())


def unturn(dq, own, others, cosine, sine, x, after):
    n, width = x.shape
    count = dq.shape[0]
    pair = pl.BlockSpec((1, count, n), lambda i: (jnp.maximum(i - 1, 0), 0, 0))
    table = whole_block(HEAD_DIM // 2, n)
    return pl.pallas_call(
        functools.partial(unturn_kernel, len(others)),
        grid=(3,),
        in_specs=[whole_block(count, n), pair] + [pair] * len(others) + [table, table, whole_block(n, width)]
        + [pl.BlockSpec(memory_space=pl.ANY)] * len(after),
        out_specs=[
            pl.BlockSpec((1, count, n), lambda i: (i, 0, 0)),
            pl.BlockSpec((1, count, width), lambda i: (i, 0, 0)),
        ],
        out_shape=[
            jax.ShapeDtypeStruct((3, count, n), LOW),
            jax.ShapeDtypeStruct((3, count, width), LOW),
        ],
        compiler_params=pltpu.CompilerParams(vmem_limit_bytes=30 << 20),
        cost_estimate=cost(flops=6 * n * width * count, bytes_accessed=9 << 20, transcendentals=0),
        name="unturn",
    )(dq, own, *others, cosine, sine, x, *after)


def finish_kernel(groups, *refs):
    res_ref, w_ref = refs[groups : groups + 2]
    in_ref = refs[-1]
    grad = jnp.concatenate([r[kind] for kind in range(3) for r in refs[:groups]], axis=0)
    in_ref[...] = (res_ref[...] + dot(grad, w_ref[...], 0, 0)).astype(LOW)


def finish(grads, resid, qkv_t, after, part, n):
    width = resid.shape[1]
    step = min(n, 256)
    first = part * (n // step)
    rows = pl.BlockSpec((step, width), lambda i: (i + first, 0))
    return pl.pallas_call(
        functools.partial(finish_kernel, len(grads)),
        grid=(n // step,),
        in_specs=[pl.BlockSpec((3, a.shape[1], step), lambda i: (0, 0, i + first)) for a in grads]
        + [rows, pl.BlockSpec(qkv_t.shape, lambda i: (0, 0), pipeline_mode=pl.Buffered(1))]
        + [pl.BlockSpec(memory_space=pl.ANY)] * len(after),
        out_specs=pl.BlockSpec((step, width), lambda i: (i, 0)),
        out_shape=jax.ShapeDtypeStruct((n, width), LOW),
        compiler_params=pltpu.CompilerParams(vmem_limit_bytes=50 << 20),
        cost_estimate=cost(flops=6 * n * width * width, bytes_accessed=12 << 20, transcendentals=0),
        name="finish",
    )(*grads, resid, qkv_t, *after)


def beside_kernel(count, *refs):
    out = refs[-1]
    at = 0
    for ref in refs[:count]:
        n = ref.shape[1]
        out[:, at : at + n] = ref[...]
        at += n


def beside(arrays, after):
    whole = pl.BlockSpec(memory_space=pltpu.VMEM)
    total = sum(a.shape[1] for a in arrays)
    return pl.pallas_call(
        functools.partial(beside_kernel, len(arrays)),
        in_specs=[whole] * len(arrays) + [pl.BlockSpec(memory_space=pl.ANY)] * len(after),
        out_specs=whole,
        out_shape=jax.ShapeDtypeStruct((arrays[0].shape[0], total), arrays[0].dtype),
        name="beside",
    )(*arrays, *after)


def select_kernel(at, x_ref, *refs):
    outs = refs[-x_ref.shape[0] :]
    for k, out in enumerate(outs):
        out[...] = x_ref[at[k]]


def select(x, at, after):
    count = x.shape[0]
    whole = pl.BlockSpec(memory_space=pltpu.VMEM)
    return pl.pallas_call(
        select_kernel,
        in_specs=[pl.BlockSpec(memory_space=pltpu.SMEM), whole] + [pl.BlockSpec(memory_space=pl.ANY)] * len(after),
        out_specs=[whole] * count,
        out_shape=[jax.ShapeDtypeStruct(x.shape[1:], x.dtype)] * count,
        compiler_params=pltpu.CompilerParams(vmem_limit_bytes=10 << 20),
        cost_estimate=cost(flops=0, bytes_accessed=4 * x.size, transcendentals=0),
        name="select",
    )(at, x, *after)


def stack_kernel(count, *refs):
    out = refs[-1]
    at = 0
    for ref in refs[:count]:
        n = ref.shape[0]
        out[at : at + n] = ref[...]
        at += n


def stack(arrays, after=()):
    one = arrays[0]
    total = sum(a.shape[0] for a in arrays)
    whole = pl.BlockSpec(memory_space=pltpu.VMEM)
    return pl.pallas_call(
        functools.partial(stack_kernel, len(arrays)),
        in_specs=[whole] * len(arrays) + [pl.BlockSpec(memory_space=pl.ANY)] * len(after),
        out_specs=whole,
        out_shape=jax.ShapeDtypeStruct((total,) + one.shape[1:], one.dtype),
        compiler_params=pltpu.CompilerParams(vmem_limit_bytes=16 << 20),
        cost_estimate=cost(bytes_accessed=4 * one.size * len(arrays)),
        name="stack",
    )(*arrays, *after)


def arrange_kernel(cuts, place, mine, theirs, *refs):
    near, depth = mine.shape[:2]
    for half, src in enumerate((mine, theirs)):
        for r in range(near):
            spot = place[half * near + r]
            for k in range(depth):
                z = place[2 * near + k]
                for out, (start, size, z_first) in zip(refs[-len(cuts) :], cuts):
                    block = src[r, k, start : start + size]
                    if z_first:
                        out[z, spot] = block
                    else:
                        out[spot, z] = block


def arrange(mine, theirs, place, cuts, after):
    near, depth, _, width = mine.shape
    whole = pl.BlockSpec(memory_space=pltpu.VMEM)
    lead = {True: (depth, 2 * near), False: (2 * near, depth)}
    return pl.pallas_call(
        functools.partial(arrange_kernel, cuts),
        in_specs=[pl.BlockSpec(memory_space=pltpu.SMEM), whole, whole]
        + [pl.BlockSpec(memory_space=pl.ANY)] * len(after),
        out_specs=[whole] * len(cuts),
        out_shape=[
            jax.ShapeDtypeStruct(lead[z_first] + (size, width), mine.dtype) for _, size, z_first in cuts
        ],
        compiler_params=pltpu.CompilerParams(vmem_limit_bytes=30 << 20),
        cost_estimate=cost(flops=0, bytes_accessed=8 * mine.size, transcendentals=0),
        name="arrange",
    )(place, mine, theirs, *after)


def add_low(a, b):
    return (a.astype(WIDE) + b.astype(WIDE)).astype(LOW)


def join_core_kernel(axis, place, mine, got, *refs):
    outs = refs[-2:]
    for i in range(4):
        for t in range(mine.shape[1 - axis]):
            spot = (place[i], t) if axis == 0 else (t, place[i])
            outs[i // 2][i % 2, t] = add_low(mine[spot], got[spot])


def join_far_kernel(keep, got, *refs):
    for i, out in enumerate(refs[-2:]):
        out[...] = add_low(keep[i], got[i])


def join_near_kernel(place, keep, got, *refs):
    for k, out in enumerate(refs[-keep.shape[0] :]):
        out[...] = add_low(keep[place[k]], got[place[k]])


def join(kernel, arrays, shapes, after, scalars=()):
    whole = pl.BlockSpec(memory_space=pltpu.VMEM)
    return pl.pallas_call(
        kernel,
        in_specs=[pl.BlockSpec(memory_space=pltpu.SMEM)] * len(scalars)
        + [whole] * len(arrays)
        + [pl.BlockSpec(memory_space=pl.ANY)] * len(after),
        out_specs=[whole] * len(shapes),
        out_shape=[jax.ShapeDtypeStruct(shape, LOW) for shape in shapes],
        compiler_params=pltpu.CompilerParams(vmem_limit_bytes=24 << 20),
        cost_estimate=cost(bytes_accessed=8 * arrays[0].size),
        name="join",
    )(*scalars, *arrays, *after)


def side_kernel(pieces, core_ref, mix_ref, hid_ref, proj_ref, *refs):
    att_refs = refs[:pieces]
    norm_ref, mine, send, turned, result, side = refs[pieces:]
    j = pl.program_id(0)
    lines, count = mine.shape[2], mix_ref.shape[1] // (2 * mine.shape[1])
    extra = norm_ref.shape[0]
    few = lines - count - extra

    @pl.when(j == 0)
    def _():
        turned[...] = mix_ref[...].T
        side[...] = dot(proj_ref[...].T, jnp.concatenate([r[...] for r in att_refs], axis=0), 1, 1)

    result[...] = dot(turned[...], hid_ref[0], 1, 0)
    for p in range(mine.shape[1]):
        for rel, out in enumerate((mine, send)):
            dp = 2 * p + (core_ref[0] + rel) % 2
            rows = result[pl.ds(pl.multiple_of(dp * count, 8), count)]
            small = side[pl.ds(pl.multiple_of((dp * pl.num_programs(0) + j) * few, 8), few)]
            out[0, p, :count] = rows.astype(LOW)
            out[0, p, count:] = jnp.concatenate([small, norm_ref[...]], axis=0).astype(LOW)


def side_grads(core, mix_grad, hidden, proj_grad, attended, norms, lines, chips):
    n, width = mix_grad.shape
    blocks = hidden.shape[0]
    whole = pl.BlockSpec((n, width), lambda j: (0, 0))
    out = pl.BlockSpec((1, chips, lines, width), lambda j: (j, 0, 0, 0))
    return pl.pallas_call(
        functools.partial(side_kernel, len(attended)),
        grid=(blocks,),
        in_specs=[
            pl.BlockSpec(memory_space=pltpu.SMEM),
            whole,
            pl.BlockSpec((1, n, width), lambda j: (j, 0, 0)),
            whole,
        ]
        + [whole_block(*a.shape) for a in attended]
        + [whole_block(8, width)],
        out_specs=[out] * 2,
        out_shape=[jax.ShapeDtypeStruct((blocks, chips, lines, width), LOW)] * 2,
        scratch_shapes=[
            pltpu.VMEM((width, n), LOW),
            pltpu.VMEM((width, width), WIDE),
            pltpu.VMEM((width, width), WIDE),
        ],
        compiler_params=pltpu.CompilerParams(vmem_limit_bytes=40 << 20),
        cost_estimate=cost(flops=10 * n * width * width, bytes_accessed=16 << 20),
        name="side_grads",
    )(core.reshape(1), *far(mix_grad, hidden, proj_grad, *attended), norms)


def gate_up_kernel(x_ref, g_ref, *refs):
    out, turned = refs[-2:]

    @pl.when(pl.program_id(0) == 0)
    def _():
        turned[...] = x_ref[...].T

    made = dot(turned[...], g_ref[0], 1, 0).astype(LOW)
    out[...] = made.reshape(out.shape)


def gate_up_grads(x, grads, first, count, given, after, ways):
    n, width = x.shape
    blocks, _, both = grads.shape
    free = pl.BlockSpec(memory_space=pl.ANY)
    return pl.pallas_call(
        gate_up_kernel,
        grid=(count,),
        in_specs=[
            pl.BlockSpec((n, width), lambda j: (0, 0)),
            pl.BlockSpec((1, n, both), lambda j: (j + first, 0, 0)),
        ]
        + [free] * (len(given) + len(after)),
        out_specs=pl.BlockSpec((ways, 1, width // ways, both), lambda j: (0, j + first, 0, 0)),
        out_shape=pltpu.HBM((ways, blocks, width // ways, both), LOW),
        input_output_aliases={2: 0} if given else {},
        scratch_shapes=[pltpu.VMEM((width, n), LOW)],
        compiler_params=pltpu.CompilerParams(vmem_limit_bytes=40 << 20),
        cost_estimate=cost(flops=2 * n * width * count * both, bytes_accessed=12 << 20, scale=1),
        name="gate_up_grads",
    )(*far(x, grads, *given), *after)


def local(
    tp, ways, tokens, segment_ids, positions, w_qkv, w_out, norm1_gain, norm1_shift, w_gate, w_up, w_down, norm2_gain, norm2_shift, out_grad
):
    rows, piece, width = tokens.shape
    chips, per_group = ways
    dp, near = 2 * chips, tp // per_group
    line = ("core", "zg", "zm")
    flat = ("zg", "zm")
    everyone = ("zg", "zm", "chip", "core")
    core = lax.axis_index("core")
    chip = lax.axis_index("chip")
    group = lax.axis_index("zg")
    z = group * near + lax.axis_index("zm")
    member = lax.axis_index("zm") * 2 + core
    own = rows * piece
    by_hand = chips == 4 and tp == 4

    def ring(step):
        pairs = []
        for c in range(2):
            for j in range(tp):
                row = c * rows + (j + step) % rows
                m = j // rows
                pairs.append((c * tp + j, (m % 2) * tp + row * near + m // 2))
        return pairs

    def bring(x, after=()):
        at = jnp.stack([(z + k) % rows for k in range(rows)]).astype(jnp.int32)
        return [lax.ppermute(a, line, ring(k)) for k, a in enumerate(select(x, at, after))]

    def send_back(parts):
        return [lax.ppermute(part, line, [(b, a) for a, b in ring(k)]) for k, part in enumerate(parts)]

    def settle(back):
        return jnp.roll(jnp.stack(back), z, axis=0)

    def give_back(parts):
        return settle(send_back(parts))

    def hop(x, first):
        pairs = []
        for p in range(4):
            for c in range(2):
                bit = 1 if (c == 0) == first else 2
                pairs.append((p * 2 + c, (p ^ bit) * 2 + c))
        return lax.ppermute(x, ("chip", "core"), pairs)

    def along(x, k):
        return lax.ppermute(x, flat, [(i, (i + k) % tp) for i in range(tp)])

    mask_one, mask_two = jnp.where(core == 0, 1, 2), jnp.where(core == 0, 2, 1)

    def spread_z(x, after=()):
        return stack([x[None]] + [along(x, k)[None] for k in range(1, tp)], after) if by_hand else x

    def spread_near(column, after=()):
        return stack([column, hop(column, True)], after) if by_hand else column

    def spread_far(pair, after=()):
        return stack([pair, hop(pair, False)], after) if by_hand else pair

    def spread_core(mine, cuts, after=()):
        if not by_hand:
            whole = lax.all_gather(mine, everyone, axis=0, tiled=False).reshape((tp, dp) + mine.shape)
            parts = [(whole[:, :, at : at + size], z_first) for at, size, z_first in cuts]
            return [a if z_first else a.swapaxes(0, 1) for a, z_first in parts]
        theirs = lax.ppermute(mine, "core", SWAP)
        place = [(chip ^ m) * 2 + core for m in (0, mask_one, mask_two, 3)]
        place += [(chip ^ m) * 2 + 1 - core for m in (0, mask_two, mask_one, 3)]
        place += [(z - k) % tp for k in range(tp)]
        mine, theirs = (a.reshape((chips, tp) + a.shape[1:]) for a in (mine, theirs))
        return arrange(mine, theirs, jnp.stack(place).astype(jnp.int32), cuts, after)

    def gather_all(x):
        return lax.all_gather(x, everyone, axis=0, tiled=False).reshape((tp, dp) + x.shape)

    pick = lambda a, i, axis: lax.dynamic_index_in_dim(a, i, axis, False)
    near_place = jnp.stack([chip, chip ^ mask_one, chip ^ mask_two, chip ^ 3]).astype(jnp.int32)
    line_place = jnp.stack([(z + k) % tp for k in range(tp)]).astype(jnp.int32)

    def collapse_core(mine, send, axis, after=()):
        got = lax.ppermute(send, "core", SWAP)
        shape = (2,) + mine.shape[: axis] + mine.shape[axis + 1 :]
        return join(functools.partial(join_core_kernel, axis), [mine, got], [shape] * 2, after, (near_place,))

    def collapse_far(keep, send, after=()):
        return join(join_far_kernel, [keep, hop(send, False)], [keep.shape[1:]] * 2, after)

    def collapse_near(keep, send, after=()):
        return join(join_near_kernel, [keep, hop(send, True)], [keep.shape[1:]] * tp, after, (line_place,))

    def collapse_z(parts):
        total = parts[0].astype(WIDE)
        for k in range(1, tp):
            total += along(parts[k], k).astype(WIDE)
        return total

    def collapse_all(x):
        return lax.psum_scatter(
            x.reshape((tp * dp,) + x.shape[2:]), everyone, scatter_dimension=0, tiled=False
        ).astype(WIDE)

    nq, no = w_qkv.shape[1], w_out.shape[1]
    units = w_gate.shape[1]
    blocks = tp * units // width
    merged = by_hand and units == width
    me = (chip * 2 + core) * tp + z
    mine_at = me * no
    vector_rows = jnp.stack([norm1_gain, norm1_shift, norm2_gain, norm2_shift])
    if merged:
        placed = jnp.where(jnp.arange(width) // no == me, jnp.tile(vector_rows, (1, dp * tp)), 0)
        small = jnp.concatenate([w_out.T, placed, jnp.zeros((4, width), LOW)])
    brought = bring(tokens)
    x = jnp.concatenate(brought)
    column = spread_z(w_qkv.T, tuple(brought[:1]))
    qkv_t = spread_core(spread_far(spread_near(column), tuple(brought[1:])), [(0, nq, False)])[0]
    qkv_t = qkv_t.reshape(3 * width, width)
    if merged:
        pack = gather_all(stack([w_gate, w_up, w_down.T, small]))
        small = ()
    else:
        regroup = lambda a: a.reshape(blocks, tp // blocks, width, units).swapaxes(1, 2).reshape(blocks, dp, -1, width)
        pack = jnp.concatenate([regroup(gather_all(a)) for a in (w_gate, w_up, w_down.T)], axis=2)
        out_t = gather_all(w_out.T).swapaxes(0, 1).reshape(width, width)
        vectors = gather_all(vector_rows).swapaxes(0, 1).reshape(dp * tp, 4, no).swapaxes(0, 1)
        small = (out_t, jnp.pad(vectors.reshape(4, width).astype(WIDE), ((0, 4), (0, 0))))

    info = jnp.stack([segment_ids, positions])
    other = lax.ppermute(info, "core", SWAP)
    info = jnp.where(core == 0, jnp.stack([info, other], 1), jnp.stack([other, info], 1))
    info = info.reshape(2, 2 * rows, -1)
    info = lax.dynamic_index_in_dim(info, group, 1, False)
    second = (info[0] != info[0, 0]).reshape(-1, rows, piece)
    second = jnp.roll(second[:, ::-1], group + 1, axis=1).reshape(-1, own)
    places = info[1].reshape(-1, rows, piece)
    places = jnp.roll(places[:, ::-1], group + 1, axis=1).reshape(-1, own)
    own_second = lax.dynamic_index_in_dim(second, member, 0, False)
    own_places = lax.dynamic_index_in_dim(places, member, 0, False)

    def key_aug(is_second):
        return jnp.pad(
            jnp.stack([jnp.where(is_second, 0.0, -MASK), jnp.where(is_second, -MASK, 0.0)]), ((0, AUG - 2), (0, 0))
        ).astype(LOW)

    query_aug = jnp.pad(
        jnp.stack([own_second, ~own_second]).astype(WIDE), ((0, AUG - 2), (0, 0))
    ).astype(LOW)

    half = HEAD_DIM // 2
    frequency = 1000.0 ** (-(jnp.arange(half, dtype=WIDE) * 2.0) / HEAD_DIM)
    angles = own_places.astype(WIDE)[None] * frequency[:, None]
    cosine, sine = jnp.cos(angles), jnp.sin(angles)

    kv = project(qkv_t, x, cosine, sine, "kv", 1)
    members = 2 * near
    if members == 2:
        kvs = [kv, lax.ppermute(kv, "core", SWAP)]
        other_second = lax.dynamic_index_in_dim(second, 1 - member, 0, False)
        kas = [key_aug(own_second), key_aug(other_second)]
        types = [WIDE, LOW]
    else:
        kvs = [lax.all_gather(kv, ("zm", "core"), axis=1, tiled=True)]
        kas = [key_aug(second.reshape(-1))]
        types = [LOW]
    q = project(qkv_t, x, cosine, sine, "q", 0)
    spans = [(i * HEADS // PIECES, HEADS // PIECES) for i in range(PIECES)]
    top_parts = bring(out_grad, tuple(far(kv)))
    attended, lse = attend_forward(q, query_aug, kvs, kas, (), 0, HEADS)
    grad_top = stack(top_parts, tuple(far(attended)))

    (x_low, hidden, gug, mix_grad, d_resid_one, proj_grad, att_grad, sums), output = middle(
        attended, x, grad_top, pack, small, rows
    )
    returned = send_back(output)
    output = settle(returned)

    def ungroup(g):
        g = g.reshape(blocks, width, tp // blocks, units).swapaxes(1, 2)
        return g.reshape(tp, dp, width // dp, units)

    if merged:
        mine, send = side_grads(core, mix_grad, hidden, proj_grad, [attended], sums, width // dp + no + 8, chips)
    else:
        g_out = dot(proj_grad, attended, 0, 1).astype(LOW).reshape(dp, tp, no, width)
        spread_sums = jnp.broadcast_to(sums.astype(LOW), (dp, tp, 8, width))
        side = collapse_all(jnp.concatenate([g_out, spread_sums], axis=2).swapaxes(0, 1))
        g_down = jnp.einsum("td,jtf->jdf", mix_grad, hidden, preferred_element_type=WIDE).astype(LOW)
        g_down = collapse_all(ungroup(g_down))
        mine = mix_grad
    split = blocks // 2
    g_gu = gate_up_grads(x_low, gug, 0, split, (), (mine,), dp)
    held = ()
    if merged:
        held = collapse_core(mine, send, 1, tuple(far(g_gu)))
    g_gu = gate_up_grads(x_low, gug, split, blocks - split, (g_gu,), tuple(held), dp)
    g_gu = g_gu.reshape(dp, blocks, width // dp, 2, tp // blocks, units).transpose(0, 1, 4, 2, 3, 5)
    g_gu = g_gu.reshape(dp, tp, width // dp, 2 * units)
    shared_gu = lax.psum_scatter(g_gu, ("chip", "core"), scatter_dimension=0, tiled=False)
    shared_gu = lax.psum_scatter(shared_gu, flat, scatter_dimension=0, tiled=False).astype(WIDE)
    spans = [(i * HEADS // PIECES, HEADS // PIECES) for i in range(PIECES)]

    dqs, grads, parts = [], [], []
    for i, (start, count) in enumerate(spans):
        after = tuple(held) + (tuple(far(g_gu)) if i == 0 else ()) + (tuple(far(*returned)) if i == 1 else ())
        dq, dkv = attend_backward(q, att_grad, attended, lse, query_aug, kvs, kas, types, after, start, count)
        if merged and i == 0:
            held = collapse_far(*held, (dq,))
        if merged and i == 1:
            held = collapse_near(*held, (dq,))
        if merged and i == 2:
            total = collapse_z(held)
            held = (total,)
        if members == 2:
            own_dkv, others = dkv[0], (lax.ppermute(dkv[1], "core", SWAP),)
        else:
            summed = lax.psum_scatter(dkv[0], ("zm", "core"), scatter_dimension=2, tiled=True)
            own_dkv, others = summed.astype(WIDE), ()
        dqs.append((dq, own_dkv, others))
    for i, (dq, own_dkv, others) in enumerate(dqs):
        grad, part = unturn(dq, own_dkv, others, cosine, sine, x, ())
        grads.append(grad)
        parts.append(part)
    if merged:
        g_down, side = total[: width // dp], total[width // dp :]
    g_qkv = jnp.concatenate(parts, axis=1).reshape(dp, tp, nq, width)
    if not by_hand:
        g_qkv = collapse_all(g_qkv.swapaxes(0, 1))
        in_grad = finish(grads, d_resid_one, qkv_t, (), 0, own)
        in_grad = give_back([in_grad[k * piece : (k + 1) * piece] for k in range(rows)])
    else:
        g_qkv = g_qkv.reshape(chips, 2, tp, nq, width)
        mine, send = pick(g_qkv, core, 1), pick(g_qkv, 1 - core, 1)
        in_grad = [finish(grads, d_resid_one, qkv_t, (send,), 0, piece)]
        held = collapse_core(mine, send, 0, (in_grad[0],))
        for k in range(1, rows):
            in_grad.append(finish(grads, d_resid_one, qkv_t, (held[0],), k, piece))
        held = collapse_far(*held, (in_grad[-1],))
        g_qkv = collapse_z(collapse_near(*held))
        in_grad = give_back(in_grad)
    vector_grads = lax.dynamic_slice_in_dim(side[no : no + 4], mine_at, no, 1)
    return (
        output,
        in_grad,
        g_qkv.T,
        side[:no].T,
        vector_grads[0],
        vector_grads[1],
        shared_gu[:, :units],
        shared_gu[:, units:],
        g_down.T,
        vector_grads[2],
        vector_grads[3],
    )


def solution(mesh):
    dp, tp = mesh.shape["dp"], mesh.shape["tp"]

    def run(*arrays):
        rows = arrays[0].shape[0] // dp
        groups = 2 * rows
        grid = Mesh(
            mesh.devices.reshape(dp // 2, 2, groups, tp // groups), ("chip", "core", "zg", "zm")
        )
        d, t = ("chip", "core"), ("zg", "zm")
        both = d + t
        placed = (
            P(d, t, None),
            P(d, None),
            P(d, None),
            P(None, both),
            P(None, both),
            P(both),
            P(both),
            P(d, t),
            P(d, t),
            P(t, d),
            P(both),
            P(both),
            P(d, t, None),
        )
        return jax.shard_map(
            functools.partial(local, tp, (dp // 2, groups)),
            mesh=grid,
            in_specs=placed,
            out_specs=(
                P(d, t, None),
                P(d, t, None),
                P(None, both),
                P(None, both),
                P(both),
                P(both),
                P(d, t),
                P(d, t),
                P(t, d),
                P(both),
                P(both),
            ),
            check_vma=False,
        )(*arrays)

    return run
```

```python
import functools

import jax
import jax.numpy as jnp
from jax import lax
from jax.experimental import pallas as pl
from jax.experimental.pallas import tpu as pltpu
import numpy as np
from jax.sharding import Mesh, PartitionSpec as P

HEADS = 12
HEAD_DIM = 64
EPSILON = 1e-05
AUG = 16
PIECES = 4
COST = 16
CHUNK = 512
MASK = 2.0**99
LOW = jnp.bfloat16
WIDE = jnp.float32
SWAP = [(0, 1), (1, 0)]


def dot(a, b, ca, cb):
    return lax.dot_general(a, b, (((ca,), (cb,)), ((), ())), preferred_element_type=WIDE)


def cost(flops=0, bytes_accessed=0, transcendentals=0, scale=COST):
    return pl.CostEstimate(
        flops=flops // scale, bytes_accessed=bytes_accessed // scale, transcendentals=transcendentals // scale
    )


def far(*arrays):
    return [pltpu.with_memory_space_constraint(a, pltpu.HBM) for a in arrays]


def split3(x):
    high = x.astype(LOW)
    rest = x - high.astype(WIDE)
    middle = rest.astype(LOW)
    return [high, middle, (rest - middle.astype(WIDE)).astype(LOW)]


def put_rows(base, at, rows):
    index = lax.broadcasted_iota(jnp.int32, base.shape, 0)
    out = base.astype(WIDE)
    for i, row in enumerate(rows):
        out = jnp.where(index == at + i, row.astype(WIDE), out)
    return out.astype(LOW)


def ones_row(n):
    return jnp.ones((1, n), WIDE)


def forward_kernel(parts, *refs):
    q_ref, qa_ref = refs[:2]
    refs = refs[: 2 + 3 * parts] + refs[-3:]
    k_refs, v_refs, ka_refs = refs[2 : 2 + parts], refs[2 + parts : 2 + 2 * parts], refs[2 + 2 * parts : 2 + 3 * parts]
    o_ref, lse_ref, keys = refs[2 + 3 * parts :]
    at = 0
    values = []
    for k_ref, v_ref, ka_ref in zip(k_refs, v_refs, ka_refs):
        n = k_ref.shape[1]
        keys[at : at + n] = jnp.concatenate([k_ref[...], ka_ref[...]], axis=0).T
        values.append(v_ref[...])
        at += n
    queries = jnp.concatenate([q_ref[...], qa_ref[...]], axis=0)
    scores = dot(keys[...], queries, 1, 0)
    top = jnp.max(scores, axis=0, keepdims=True)
    terms = jnp.exp(scores - top)
    total = jnp.sum(terms, axis=0, keepdims=True)
    result = dot(jnp.concatenate(values, axis=1), terms.astype(LOW), 1, 0)
    o_ref[...] = (result / total).astype(LOW)
    lse_ref[...] = (top + jnp.log(total)).reshape(1, 1, -1)


def head_block(n, first):
    return pl.BlockSpec((HEAD_DIM, n), lambda h: (h + first, 0))


def whole_block(rows, n):
    return pl.BlockSpec((rows, n), lambda h: (0, 0))


def attend_forward(q, qa, kvs, kas, after, first, heads):
    parts, nq = len(kvs), q.shape[1]
    sizes = [kv.shape[1] for kv in kvs]
    nk = sum(sizes)
    return pl.pallas_call(
        functools.partial(forward_kernel, parts),
        grid=(heads,),
        in_specs=[head_block(nq, first), whole_block(AUG, nq)]
        + [head_block(n, first) for n in sizes]
        + [head_block(n, first + HEADS) for n in sizes]
        + [whole_block(AUG, n) for n in sizes]
        + [pl.BlockSpec(memory_space=pl.ANY)] * len(after),
        out_specs=[head_block(nq, 0), pl.BlockSpec((1, 1, nq), lambda h: (h, 0, 0))],
        out_shape=[
            jax.ShapeDtypeStruct((heads * HEAD_DIM, nq), LOW),
            jax.ShapeDtypeStruct((heads, 1, nq), WIDE),
        ],
        scratch_shapes=[pltpu.VMEM((nk, HEAD_DIM + AUG), LOW)],
        compiler_params=pltpu.CompilerParams(vmem_limit_bytes=28 << 20),
        cost_estimate=cost(
            flops=16 * heads * nq * nk * HEAD_DIM,
            bytes_accessed=4 * heads * HEAD_DIM * (nq + nk),
            transcendentals=heads * nq * nk,
        ),
        name="attend_forward",
    )(*far(q), qa, *far(*kvs), *far(*kvs), *kas, *after)


def backward_kernel(parts, *refs):
    q_ref, g_ref, o_ref, lse_ref, qa_ref = refs[:5]
    refs = refs[: 5 + 3 * parts] + refs[-3 - parts :]
    k_refs, v_refs, ka_refs = refs[5 : 5 + parts], refs[5 + parts : 5 + 2 * parts], refs[5 + 2 * parts : 5 + 3 * parts]
    dq_ref = refs[5 + 3 * parts]
    dkv_refs = refs[6 + 3 * parts : 6 + 4 * parts]
    keys, values = refs[6 + 4 * parts :]
    nq = q_ref.shape[1]
    at = 0
    for k_ref, v_ref, ka_ref in zip(k_refs, v_refs, ka_refs):
        n = k_ref.shape[1]
        keys[at : at + n] = jnp.concatenate(
            [k_ref[...], put_rows(ka_ref[...], 2, [ones_row(n)] * 3)], axis=0
        ).T
        values[at : at + n] = jnp.concatenate(
            [v_ref[...], put_rows(jnp.zeros((AUG, n), LOW), 0, [ones_row(n)] * 3)], axis=0
        ).T
        at += n
    grads, queries = g_ref[...], q_ref[...]
    delta = jnp.sum(grads.astype(WIDE) * o_ref[...].astype(WIDE), axis=0, keepdims=True)
    query_aug = jnp.concatenate([queries, put_rows(qa_ref[...], 2, split3(-lse_ref[0]))], axis=0)
    grad_aug = jnp.concatenate([grads, put_rows(jnp.zeros((AUG, nq), LOW), 0, split3(-delta))], axis=0)
    at = 0
    dq = jnp.zeros((HEAD_DIM, nq), WIDE)
    for k_ref, dkv_ref in zip(k_refs, dkv_refs):
        n = k_ref.shape[1]
        step = min(n, CHUNK)
        for start in range(0, n, step):
            lines = slice(at, at + step)
            spot = slice(start, start + step)
            probs = jnp.exp(dot(keys[lines], query_aug, 1, 0))
            prob_grads = dot(values[lines], grad_aug, 1, 0)
            score_grads = (probs * prob_grads).astype(LOW)
            dq += dot(k_ref[:, spot], score_grads, 1, 0)
            dkv_ref[0, :, spot] = dot(score_grads, queries, 1, 1).T.astype(dkv_ref.dtype)
            dkv_ref[1, :, spot] = dot(probs.astype(LOW), grads, 1, 1).T.astype(dkv_ref.dtype)
            at += step
    dq_ref[...] = dq * HEAD_DIM ** (-0.5)


def attend_backward(q, g, o, lse, qa, kvs, kas, types, after, first, heads):
    parts, nq = len(kvs), q.shape[1]
    sizes = [kv.shape[1] for kv in kvs]
    nk = sum(sizes)
    width = heads * HEAD_DIM
    out = pl.pallas_call(
        functools.partial(backward_kernel, parts),
        grid=(heads,),
        in_specs=[
            head_block(nq, first),
            head_block(nq, first),
            head_block(nq, first),
            pl.BlockSpec((1, 1, nq), lambda h: (h + first, 0, 0)),
            whole_block(AUG, nq),
        ]
        + [head_block(n, first) for n in sizes]
        + [head_block(n, first + HEADS) for n in sizes]
        + [whole_block(AUG, n) for n in sizes]
        + [pl.BlockSpec(memory_space=pl.ANY)] * len(after),
        out_specs=[head_block(nq, 0)]
        + [pl.BlockSpec((2, HEAD_DIM, n), lambda h: (0, h, 0)) for n in sizes],
        out_shape=[jax.ShapeDtypeStruct((width, nq), WIDE)]
        + [jax.ShapeDtypeStruct((2, width, n), t) for n, t in zip(sizes, types)],
        scratch_shapes=[pltpu.VMEM((nk, HEAD_DIM + AUG), LOW)] * 2,
        compiler_params=pltpu.CompilerParams(vmem_limit_bytes=24 << 20),
        cost_estimate=cost(
            flops=30 * heads * nq * nk * HEAD_DIM,
            bytes_accessed=8 * width * (nq + nk),
            transcendentals=heads * nq * nk,
        ),
        name="attend_backward",
    )(*far(q, g, o), lse, qa, *far(*kvs), *far(*kvs), *kas, *after)
    return out[0], out[1:]


def turn(values, cosine, sine):
    heads = values.reshape(-1, HEAD_DIM, values.shape[-1])
    half = HEAD_DIM // 2
    front, behind = heads[:, :half], heads[:, half:]
    turned = jnp.concatenate([front * cosine - behind * sine, behind * cosine + front * sine], axis=1)
    return turned.reshape(values.shape)


def project_kernel(kinds, w_ref, x_ref, cos_ref, sin_ref, o_ref):
    made = dot(w_ref[...], x_ref[...], 1, 1)
    for i, kind in enumerate(kinds):

        @pl.when(pl.program_id(0) == i)
        def _():
            if kind == "v":
                o_ref[...] = made.astype(LOW)
            else:
                low = turn(made, cos_ref[...], sin_ref[...]).astype(LOW)
                o_ref[...] = low * jnp.asarray(HEAD_DIM ** (-0.5), LOW) if kind == "q" else low


def project(qkv_t, x, cosine, sine, kinds, first):
    n, width = x.shape
    return pl.pallas_call(
        functools.partial(project_kernel, kinds),
        grid=(len(kinds),),
        in_specs=[
            pl.BlockSpec((width, width), lambda i: (i + first, 0)),
            pl.BlockSpec((n, width), lambda i: (0, 0)),
            whole_block(HEAD_DIM // 2, n),
            whole_block(HEAD_DIM // 2, n),
        ],
        out_specs=pl.BlockSpec((width, n), lambda i: (i, 0)),
        out_shape=jax.ShapeDtypeStruct((len(kinds) * width, n), LOW),
        compiler_params=pltpu.CompilerParams(vmem_limit_bytes=40 << 20),
        cost_estimate=cost(
            flops=2 * len(kinds) * width * width * n, bytes_accessed=6 * width * n, transcendentals=0
        ),
        name="project",
    )(qkv_t, x, cosine, sine)


def norm_forward(values, gain, shift):
    center = jnp.mean(values, axis=-1, keepdims=True)
    centered = values - center
    inverse = lax.rsqrt(jnp.mean(centered * centered, axis=-1, keepdims=True) + EPSILON)
    normed = centered * inverse
    return (normed * gain + shift, normed, inverse)


def norm_backward(grads, normed, inverse, gain):
    scaled = grads * gain
    first_mean = jnp.mean(scaled, axis=-1, keepdims=True)
    second_mean = jnp.mean(scaled * normed, axis=-1, keepdims=True)
    return inverse * (scaled - first_mean - normed * second_mean)


def middle_kernel(parts, few, *refs):
    att_in, x_ref, top_ref, pack = refs[:4]
    low_ref, hid_ref, gug_ref, mix_ref, res_ref, proj_ref, att_ref, sums_ref = refs[-12 - parts : -4 - parts]
    o_refs, kept, wide, out_w, vec_ref = refs[-4 - parts : -4], *refs[-4:]
    blocks, width = pack.shape[0], pack.shape[3]
    lines = width // pack.shape[1]
    if few:

        @pl.when(pl.program_id(0) == 0)
        def _():
            total = jnp.zeros((8, width), WIDE)
            for j in range(blocks):
                for i in range(pack.shape[1]):
                    rows = refs[4][j, i].astype(WIDE)
                    spot = (i * blocks + j) * few
                    wide[spot : spot + few] = rows[:few]
                    total += rows[few : few + 8]
            out_w[...] = wide[...].astype(LOW)
            vec_ref[...] = total

    else:
        out_w, vec_ref = refs[4:6]
    gain_one, shift_one, gain_two, shift_two = (vec_ref[i : i + 1] for i in range(4))

    def weight(j, kind):
        return pack[j, :, kind * lines : (kind + 1) * lines].reshape(width, width)

    projected = dot(att_in[...], out_w[...], 0, 1)
    x_one, normed_one, inverse_one = norm_forward(x_ref[...].astype(WIDE) + projected, gain_one, shift_one)
    x_low = x_one.astype(LOW)
    low_ref[...] = x_low
    mixed = jnp.zeros_like(x_one)
    for j in range(blocks):
        gate = dot(x_low, weight(j, 0), 1, 0)
        up = dot(x_low, weight(j, 1), 1, 0)
        sigma = 0.5 * jnp.tanh(0.5 * gate) + 0.5
        activated = gate * sigma
        kept[j, :, :width] = up * (sigma + activated * (1.0 - sigma))
        kept[j, :, width:] = activated
        hidden = (activated * up).astype(LOW)
        hid_ref[j] = hidden
        mixed += dot(hidden, weight(j, 2), 1, 1)
    result, normed_two, inverse_two = norm_forward(x_one + mixed, gain_two, shift_two)
    steps = pl.num_programs(0) // parts
    for k, o_ref in enumerate(o_refs):

        @pl.when(pl.program_id(0) // steps == k)
        def _():
            o_ref[...] = result.astype(LOW)

    grad_top = top_ref[...].astype(WIDE)
    d_resid_two = norm_backward(grad_top, normed_two, inverse_two, gain_two)
    mix_grad = d_resid_two.astype(LOW)
    mix_ref[...] = mix_grad
    d_x_one = d_resid_two
    for j in range(blocks):
        hidden_grad = dot(mix_grad, weight(j, 2), 1, 0)
        gate_grad = (hidden_grad * kept[j, :, :width]).astype(LOW)
        up_grad = (hidden_grad * kept[j, :, width:]).astype(LOW)
        gug_ref[j, :, :width] = gate_grad
        gug_ref[j, :, width:] = up_grad
        d_x_one += dot(gate_grad, weight(j, 0), 1, 1) + dot(up_grad, weight(j, 1), 1, 1)
    d_resid_one = norm_backward(d_x_one, normed_one, inverse_one, gain_one)
    res_ref[...] = d_resid_one
    proj_grad = d_resid_one.astype(LOW)
    proj_ref[...] = proj_grad
    att_ref[...] = dot(out_w[...], proj_grad, 0, 1).astype(LOW)
    sums = jnp.concatenate(
        [
            jnp.sum(v, axis=0, keepdims=True)
            for v in (d_x_one * normed_one, d_x_one, grad_top * normed_two, grad_top)
        ]
        + [jnp.zeros((4, d_x_one.shape[1]), WIDE)],
        axis=0,
    )

    @pl.when(pl.program_id(0) == 0)
    def _():
        sums_ref[...] = sums

    @pl.when(pl.program_id(0) > 0)
    def _():
        sums_ref[...] += sums


def middle(attended, x, grad_top, pack, small, parts):
    n, width = x.shape
    blocks, units = pack.shape[0], width
    step = min(n // parts, 256)
    steps = n // step // parts
    few = 0 if len(small) == 2 else width // (blocks * pack.shape[1])

    def kept_block(shape):
        return pl.BlockSpec(shape, lambda i: (0,) * len(shape), pipeline_mode=pl.Buffered(1))

    def part_block(k):
        return pl.BlockSpec((step, width), lambda i: (jnp.clip(i - k * steps, 0, steps - 1), 0))

    rows = pl.BlockSpec((step, width), lambda i: (i, 0))
    out = pl.pallas_call(
        functools.partial(middle_kernel, parts, few),
        grid=(n // step,),
        in_specs=[pl.BlockSpec((width, step), lambda i: (0, i)), rows, rows]
        + [kept_block(a.shape) for a in (pack,) + small],
        out_specs=[
            rows,
            pl.BlockSpec((blocks, step, units), lambda i: (0, i, 0)),
            pl.BlockSpec((blocks, step, 2 * units), lambda i: (0, i, 0)),
            rows,
            rows,
            rows,
            pl.BlockSpec((width, step), lambda i: (0, i)),
            pl.BlockSpec((8, width), lambda i: (0, 0)),
        ]
        + [part_block(k) for k in range(parts)],
        out_shape=[
            pltpu.HBM((n, width), LOW),
            pltpu.HBM((blocks, n, units), LOW),
            pltpu.HBM((blocks, n, 2 * units), LOW),
            pltpu.HBM((n, width), LOW),
            pltpu.HBM((n, width), WIDE),
            pltpu.HBM((n, width), LOW),
            pltpu.HBM((width, n), LOW),
            jax.ShapeDtypeStruct((8, width), WIDE),
        ]
        + [pltpu.HBM((n // parts, width), LOW)] * parts,
        scratch_shapes=[
            pltpu.VMEM((blocks, step, 2 * units), WIDE),
            pltpu.VMEM((width, width), WIDE),
            pltpu.VMEM((width, width), LOW),
            pltpu.VMEM((8, width), WIDE),
        ],
        compiler_params=pltpu.CompilerParams(vmem_limit_bytes=60 << 20),
        cost_estimate=cost(
            flops=2 * n * width * (2 * width + 6 * blocks * units), bytes_accessed=60 << 20, transcendentals=n * blocks * units
        ),
        name="middle",
    )(*far(attended, x, grad_top, pack), *small)
    return out[:8], out[8:]


def unturn_kernel(add, *refs):
    dq_ref, own_ref = refs[:2]
    cos_ref, sin_ref, x_ref = refs[2 + add : 5 + add]
    grad_ref, g_ref = refs[-2:]
    kind = pl.program_id(0)
    cosine, sine = cos_ref[...], -sin_ref[...]

    def emit(made):
        low = made.astype(LOW)
        grad_ref[0] = low
        g_ref[0] = dot(low, x_ref[...], 1, 0).astype(LOW)

    @pl.when(kind == 0)
    def _():
        emit(turn(dq_ref[...], cosine, sine))

    def total():
        return own_ref[0] + refs[2][0].astype(WIDE) if add else own_ref[0]

    @pl.when(kind == 1)
    def _():
        emit(turn(total(), cosine, sine))

    @pl.when(kind == 2)
    def _():
        emit(total())


def unturn(dq, own, others, cosine, sine, x, after):
    n, width = x.shape
    count = dq.shape[0]
    pair = pl.BlockSpec((1, count, n), lambda i: (jnp.maximum(i - 1, 0), 0, 0))
    table = whole_block(HEAD_DIM // 2, n)
    return pl.pallas_call(
        functools.partial(unturn_kernel, len(others)),
        grid=(3,),
        in_specs=[whole_block(count, n), pair] + [pair] * len(others) + [table, table, whole_block(n, width)]
        + [pl.BlockSpec(memory_space=pl.ANY)] * len(after),
        out_specs=[
            pl.BlockSpec((1, count, n), lambda i: (i, 0, 0)),
            pl.BlockSpec((1, count, width), lambda i: (i, 0, 0)),
        ],
        out_shape=[
            jax.ShapeDtypeStruct((3, count, n), LOW),
            jax.ShapeDtypeStruct((3, count, width), LOW),
        ],
        compiler_params=pltpu.CompilerParams(vmem_limit_bytes=30 << 20),
        cost_estimate=cost(flops=6 * n * width * count, bytes_accessed=9 << 20, transcendentals=0),
        name="unturn",
    )(dq, own, *others, cosine, sine, x, *after)


def finish_kernel(groups, *refs):
    res_ref, w_ref = refs[groups : groups + 2]
    in_ref = refs[-1]
    grad = jnp.concatenate([r[kind] for kind in range(3) for r in refs[:groups]], axis=0)
    in_ref[...] = (res_ref[...] + dot(grad, w_ref[...], 0, 0)).astype(LOW)


def finish(grads, resid, qkv_t, after, part, n):
    width = resid.shape[1]
    step = min(n, 256)
    first = part * (n // step)
    rows = pl.BlockSpec((step, width), lambda i: (i + first, 0))
    return pl.pallas_call(
        functools.partial(finish_kernel, len(grads)),
        grid=(n // step,),
        in_specs=[pl.BlockSpec((3, a.shape[1], step), lambda i: (0, 0, i + first)) for a in grads]
        + [rows, pl.BlockSpec(qkv_t.shape, lambda i: (0, 0), pipeline_mode=pl.Buffered(1))]
        + [pl.BlockSpec(memory_space=pl.ANY)] * len(after),
        out_specs=pl.BlockSpec((step, width), lambda i: (i, 0)),
        out_shape=jax.ShapeDtypeStruct((n, width), LOW),
        compiler_params=pltpu.CompilerParams(vmem_limit_bytes=50 << 20),
        cost_estimate=cost(flops=6 * n * width * width, bytes_accessed=12 << 20, transcendentals=0),
        name="finish",
    )(*grads, resid, qkv_t, *after)


def beside_kernel(count, *refs):
    out = refs[-1]
    at = 0
    for ref in refs[:count]:
        n = ref.shape[1]
        out[:, at : at + n] = ref[...]
        at += n


def beside(arrays, after):
    whole = pl.BlockSpec(memory_space=pltpu.VMEM)
    total = sum(a.shape[1] for a in arrays)
    return pl.pallas_call(
        functools.partial(beside_kernel, len(arrays)),
        in_specs=[whole] * len(arrays) + [pl.BlockSpec(memory_space=pl.ANY)] * len(after),
        out_specs=whole,
        out_shape=jax.ShapeDtypeStruct((arrays[0].shape[0], total), arrays[0].dtype),
        name="beside",
    )(*arrays, *after)


def select_kernel(at, x_ref, *refs):
    outs = refs[-x_ref.shape[0] :]
    for k, out in enumerate(outs):
        out[...] = x_ref[at[k]]


def select(x, at, after):
    count = x.shape[0]
    whole = pl.BlockSpec(memory_space=pltpu.VMEM)
    return pl.pallas_call(
        select_kernel,
        in_specs=[pl.BlockSpec(memory_space=pltpu.SMEM), whole] + [pl.BlockSpec(memory_space=pl.ANY)] * len(after),
        out_specs=[whole] * count,
        out_shape=[jax.ShapeDtypeStruct(x.shape[1:], x.dtype)] * count,
        compiler_params=pltpu.CompilerParams(vmem_limit_bytes=10 << 20),
        cost_estimate=cost(flops=0, bytes_accessed=4 * x.size, transcendentals=0),
        name="select",
    )(at, x, *after)


def settle_kernel(count, at, *refs):
    out = refs[-1]
    for r in range(count):
        for k in range(count):

            @pl.when(at[r] == k)
            def _():
                out[r] = refs[k][...]


def settle_late(back, at, after):
    whole = pl.BlockSpec(memory_space=pltpu.VMEM)
    return pl.pallas_call(
        functools.partial(settle_kernel, len(back)),
        in_specs=[pl.BlockSpec(memory_space=pltpu.SMEM)]
        + [whole] * len(back)
        + [pl.BlockSpec(memory_space=pl.ANY)] * len(after),
        out_specs=whole,
        out_shape=jax.ShapeDtypeStruct((len(back),) + back[0].shape, back[0].dtype),
        compiler_params=pltpu.CompilerParams(vmem_limit_bytes=10 << 20),
        cost_estimate=cost(bytes_accessed=4 * len(back) * back[0].size),
        name="settle",
    )(at, *back, *after)


def stack_kernel(count, *refs):
    out = refs[-1]
    at = 0
    for ref in refs[:count]:
        n = ref.shape[0]
        out[at : at + n] = ref[...]
        at += n


def stack(arrays, after=()):
    one = arrays[0]
    total = sum(a.shape[0] for a in arrays)
    whole = pl.BlockSpec(memory_space=pltpu.VMEM)
    return pl.pallas_call(
        functools.partial(stack_kernel, len(arrays)),
        in_specs=[whole] * len(arrays) + [pl.BlockSpec(memory_space=pl.ANY)] * len(after),
        out_specs=whole,
        out_shape=jax.ShapeDtypeStruct((total,) + one.shape[1:], one.dtype),
        compiler_params=pltpu.CompilerParams(vmem_limit_bytes=16 << 20),
        cost_estimate=cost(bytes_accessed=4 * one.size * len(arrays)),
        name="stack",
    )(*arrays, *after)


def arrange_kernel(cuts, place, mine, theirs, *refs):
    near, depth = mine.shape[:2]
    for half, src in enumerate((mine, theirs)):
        for r in range(near):
            spot = place[half * near + r]
            for k in range(depth):
                z = place[2 * near + k]
                for out, (start, size, z_first) in zip(refs[-len(cuts) :], cuts):
                    block = src[r, k, start : start + size]
                    if z_first:
                        out[z, spot] = block
                    else:
                        out[spot, z] = block


def arrange(mine, theirs, place, cuts, after):
    near, depth, _, width = mine.shape
    whole = pl.BlockSpec(memory_space=pltpu.VMEM)
    lead = {True: (depth, 2 * near), False: (2 * near, depth)}
    return pl.pallas_call(
        functools.partial(arrange_kernel, cuts),
        in_specs=[pl.BlockSpec(memory_space=pltpu.SMEM), whole, whole]
        + [pl.BlockSpec(memory_space=pl.ANY)] * len(after),
        out_specs=[whole] * len(cuts),
        out_shape=[
            jax.ShapeDtypeStruct(lead[z_first] + (size, width), mine.dtype) for _, size, z_first in cuts
        ],
        compiler_params=pltpu.CompilerParams(vmem_limit_bytes=30 << 20),
        cost_estimate=cost(flops=0, bytes_accessed=8 * mine.size, transcendentals=0),
        name="arrange",
    )(place, mine, theirs, *after)


def add_low(a, b):
    return (a.astype(WIDE) + b.astype(WIDE)).astype(LOW)


def join_core_kernel(axis, place, mine, got, *refs):
    outs = refs[-2:]
    for i in range(4):
        for t in range(mine.shape[1 - axis]):
            spot = (place[i], t) if axis == 0 else (t, place[i])
            outs[i // 2][i % 2, t] = add_low(mine[spot], got[spot])


def join_far_kernel(keep, got, *refs):
    for i, out in enumerate(refs[-2:]):
        out[...] = add_low(keep[i], got[i])


def join_near_kernel(place, keep, got, *refs):
    for k, out in enumerate(refs[-keep.shape[0] :]):
        out[...] = add_low(keep[place[k]], got[place[k]])


def join(kernel, arrays, shapes, after, scalars=()):
    whole = pl.BlockSpec(memory_space=pltpu.VMEM)
    return pl.pallas_call(
        kernel,
        in_specs=[pl.BlockSpec(memory_space=pltpu.SMEM)] * len(scalars)
        + [whole] * len(arrays)
        + [pl.BlockSpec(memory_space=pl.ANY)] * len(after),
        out_specs=[whole] * len(shapes),
        out_shape=[jax.ShapeDtypeStruct(shape, LOW) for shape in shapes],
        compiler_params=pltpu.CompilerParams(vmem_limit_bytes=24 << 20),
        cost_estimate=cost(bytes_accessed=8 * arrays[0].size),
        name="join",
    )(*scalars, *arrays, *after)


def side_kernel(pieces, core_ref, mix_ref, hid_ref, proj_ref, *refs):
    att_refs = refs[:pieces]
    norm_ref, mine, send, turned, result, side = refs[pieces:]
    j = pl.program_id(0)
    lines, count = mine.shape[2], mix_ref.shape[1] // (2 * mine.shape[1])
    extra = norm_ref.shape[0]
    few = lines - count - extra

    @pl.when(j == 0)
    def _():
        turned[...] = mix_ref[...].T
        side[...] = dot(proj_ref[...].T, jnp.concatenate([r[...] for r in att_refs], axis=0), 1, 1)

    result[...] = dot(turned[...], hid_ref[0], 1, 0)
    for p in range(mine.shape[1]):
        for rel, out in enumerate((mine, send)):
            dp = 2 * p + (core_ref[0] + rel) % 2
            rows = result[pl.ds(pl.multiple_of(dp * count, 8), count)]
            small = side[pl.ds(pl.multiple_of((dp * pl.num_programs(0) + j) * few, 8), few)]
            out[0, p, :count] = rows.astype(LOW)
            out[0, p, count:] = jnp.concatenate([small, norm_ref[...]], axis=0).astype(LOW)


def side_grads(core, mix_grad, hidden, proj_grad, attended, norms, lines, chips):
    n, width = mix_grad.shape
    blocks = hidden.shape[0]
    whole = pl.BlockSpec((n, width), lambda j: (0, 0))
    out = pl.BlockSpec((1, chips, lines, width), lambda j: (j, 0, 0, 0))
    return pl.pallas_call(
        functools.partial(side_kernel, len(attended)),
        grid=(blocks,),
        in_specs=[
            pl.BlockSpec(memory_space=pltpu.SMEM),
            whole,
            pl.BlockSpec((1, n, width), lambda j: (j, 0, 0)),
            whole,
        ]
        + [whole_block(*a.shape) for a in attended]
        + [whole_block(8, width)],
        out_specs=[out] * 2,
        out_shape=[jax.ShapeDtypeStruct((blocks, chips, lines, width), LOW)] * 2,
        scratch_shapes=[
            pltpu.VMEM((width, n), LOW),
            pltpu.VMEM((width, width), WIDE),
            pltpu.VMEM((width, width), WIDE),
        ],
        compiler_params=pltpu.CompilerParams(vmem_limit_bytes=40 << 20),
        cost_estimate=cost(flops=10 * n * width * width, bytes_accessed=16 << 20),
        name="side_grads",
    )(core.reshape(1), *far(mix_grad, hidden, proj_grad, *attended), norms)


def gate_up_kernel(x_ref, g_ref, *refs):
    out, turned = refs[-2:]

    @pl.when(pl.program_id(0) == 0)
    def _():
        turned[...] = x_ref[...].T

    made = dot(turned[...], g_ref[0], 1, 0).astype(LOW)
    out[...] = made.reshape(out.shape)


def gate_up_grads(x, grads, first, count, given, after, ways):
    n, width = x.shape
    blocks, _, both = grads.shape
    free = pl.BlockSpec(memory_space=pl.ANY)
    return pl.pallas_call(
        gate_up_kernel,
        grid=(count,),
        in_specs=[
            pl.BlockSpec((n, width), lambda j: (0, 0)),
            pl.BlockSpec((1, n, both), lambda j: (j + first, 0, 0)),
        ]
        + [free] * (len(given) + len(after)),
        out_specs=pl.BlockSpec((ways, 1, width // ways, both), lambda j: (0, j + first, 0, 0)),
        out_shape=pltpu.HBM((ways, blocks, width // ways, both), LOW),
        input_output_aliases={2: 0} if given else {},
        scratch_shapes=[pltpu.VMEM((width, n), LOW)],
        compiler_params=pltpu.CompilerParams(vmem_limit_bytes=40 << 20),
        cost_estimate=cost(flops=2 * n * width * count * both, bytes_accessed=12 << 20, scale=1),
        name="gate_up_grads",
    )(*far(x, grads, *given), *after)


def local(
    tp, ways, tokens, segment_ids, positions, w_qkv, w_out, norm1_gain, norm1_shift, w_gate, w_up, w_down, norm2_gain, norm2_shift, out_grad
):
    rows, piece, width = tokens.shape
    chips, per_group = ways
    dp, near = 2 * chips, tp // per_group
    line = ("core", "zg", "zm")
    flat = ("zg", "zm")
    everyone = ("zg", "zm", "chip", "core")
    core = lax.axis_index("core")
    chip = lax.axis_index("chip")
    group = lax.axis_index("zg")
    z = group * near + lax.axis_index("zm")
    member = lax.axis_index("zm") * 2 + core
    own = rows * piece
    by_hand = chips == 4 and tp == 4

    def ring(step):
        pairs = []
        for c in range(2):
            for j in range(tp):
                row = c * rows + (j + step) % rows
                m = j // rows
                pairs.append((c * tp + j, (m % 2) * tp + row * near + m // 2))
        return pairs

    def bring(x, after=()):
        at = jnp.stack([(z + k) % rows for k in range(rows)]).astype(jnp.int32)
        return [lax.ppermute(a, line, ring(k)) for k, a in enumerate(select(x, at, after))]

    def send_back(parts, first):
        return [lax.ppermute(part, line, [(b, a) for a, b in ring(first + k)]) for k, part in enumerate(parts)]

    def settle(back):
        return jnp.roll(jnp.stack(back), z, axis=0)

    def give_back(parts):
        return settle(send_back(parts, 0))

    def hop(x, first):
        pairs = []
        for p in range(4):
            for c in range(2):
                bit = 1 if (c == 0) == first else 2
                pairs.append((p * 2 + c, (p ^ bit) * 2 + c))
        return lax.ppermute(x, ("chip", "core"), pairs)

    def along(x, k):
        return lax.ppermute(x, flat, [(i, (i + k) % tp) for i in range(tp)])

    mask_one, mask_two = jnp.where(core == 0, 1, 2), jnp.where(core == 0, 2, 1)

    def spread_z(x, after=()):
        return stack([x[None]] + [along(x, k)[None] for k in range(1, tp)], after) if by_hand else x

    def spread_near(column, after=()):
        return stack([column, hop(column, True)], after) if by_hand else column

    def spread_far(pair, after=()):
        return stack([pair, hop(pair, False)], after) if by_hand else pair

    def spread_core(mine, cuts, after=()):
        if not by_hand:
            whole = lax.all_gather(mine, everyone, axis=0, tiled=False).reshape((tp, dp) + mine.shape)
            parts = [(whole[:, :, at : at + size], z_first) for at, size, z_first in cuts]
            return [a if z_first else a.swapaxes(0, 1) for a, z_first in parts]
        theirs = lax.ppermute(mine, "core", SWAP)
        place = [(chip ^ m) * 2 + core for m in (0, mask_one, mask_two, 3)]
        place += [(chip ^ m) * 2 + 1 - core for m in (0, mask_two, mask_one, 3)]
        place += [(z - k) % tp for k in range(tp)]
        mine, theirs = (a.reshape((chips, tp) + a.shape[1:]) for a in (mine, theirs))
        return arrange(mine, theirs, jnp.stack(place).astype(jnp.int32), cuts, after)

    def gather_all(x):
        return lax.all_gather(x, everyone, axis=0, tiled=False).reshape((tp, dp) + x.shape)

    pick = lambda a, i, axis: lax.dynamic_index_in_dim(a, i, axis, False)
    near_place = jnp.stack([chip, chip ^ mask_one, chip ^ mask_two, chip ^ 3]).astype(jnp.int32)
    line_place = jnp.stack([(z + k) % tp for k in range(tp)]).astype(jnp.int32)

    def collapse_core(mine, send, axis, after=()):
        got = lax.ppermute(send, "core", SWAP)
        shape = (2,) + mine.shape[: axis] + mine.shape[axis + 1 :]
        return join(functools.partial(join_core_kernel, axis), [mine, got], [shape] * 2, after, (near_place,))

    def collapse_far(keep, send, after=()):
        return join(join_far_kernel, [keep, hop(send, False)], [keep.shape[1:]] * 2, after)

    def collapse_near(keep, send, after=()):
        return join(join_near_kernel, [keep, hop(send, True)], [keep.shape[1:]] * tp, after, (line_place,))

    def collapse_z(parts):
        total = parts[0].astype(WIDE)
        for k in range(1, tp):
            total += along(parts[k], k).astype(WIDE)
        return total

    def collapse_all(x):
        return lax.psum_scatter(
            x.reshape((tp * dp,) + x.shape[2:]), everyone, scatter_dimension=0, tiled=False
        ).astype(WIDE)

    nq, no = w_qkv.shape[1], w_out.shape[1]
    units = w_gate.shape[1]
    blocks = tp * units // width
    merged = by_hand and units == width
    me = (chip * 2 + core) * tp + z
    mine_at = me * no
    vector_rows = jnp.stack([norm1_gain, norm1_shift, norm2_gain, norm2_shift])
    if merged:
        placed = jnp.where(jnp.arange(width) // no == me, jnp.tile(vector_rows, (1, dp * tp)), 0)
        small = jnp.concatenate([w_out.T, placed, jnp.zeros((4, width), LOW)])
    brought = bring(tokens)
    x = jnp.concatenate(brought)
    first = jnp.concatenate([small, w_qkv.T]) if merged else w_qkv.T
    extra = first.shape[0] - nq
    column = spread_z(first, tuple(brought[:1]))
    cuts = [(extra, nq, False)] + ([(0, extra, True)] if merged else [])
    qkv_t, *small = spread_core(spread_far(spread_near(column), tuple(brought[1:])), cuts)
    qkv_t = qkv_t.reshape(3 * width, width)
    if merged:
        pack = gather_all(stack([w_gate, w_up, w_down.T], (brought[0],)))
        small = tuple(far(*small))
    else:
        regroup = lambda a: a.reshape(blocks, tp // blocks, width, units).swapaxes(1, 2).reshape(blocks, dp, -1, width)
        pack = jnp.concatenate([regroup(gather_all(a)) for a in (w_gate, w_up, w_down.T)], axis=2)
        out_t = gather_all(w_out.T).swapaxes(0, 1).reshape(width, width)
        vectors = gather_all(vector_rows).swapaxes(0, 1).reshape(dp * tp, 4, no).swapaxes(0, 1)
        small = (out_t, jnp.pad(vectors.reshape(4, width).astype(WIDE), ((0, 4), (0, 0))))

    info = jnp.stack([segment_ids, positions])
    other = lax.ppermute(info, "core", SWAP)
    info = jnp.where(core == 0, jnp.stack([info, other], 1), jnp.stack([other, info], 1))
    info = info.reshape(2, 2 * rows, -1)
    info = lax.dynamic_index_in_dim(info, group, 1, False)
    second = (info[0] != info[0, 0]).reshape(-1, rows, piece)
    second = jnp.roll(second[:, ::-1], group + 1, axis=1).reshape(-1, own)
    places = info[1].reshape(-1, rows, piece)
    places = jnp.roll(places[:, ::-1], group + 1, axis=1).reshape(-1, own)
    own_second = lax.dynamic_index_in_dim(second, member, 0, False)
    own_places = lax.dynamic_index_in_dim(places, member, 0, False)

    def key_aug(is_second):
        return jnp.pad(
            jnp.stack([jnp.where(is_second, 0.0, -MASK), jnp.where(is_second, -MASK, 0.0)]), ((0, AUG - 2), (0, 0))
        ).astype(LOW)

    query_aug = jnp.pad(
        jnp.stack([own_second, ~own_second]).astype(WIDE), ((0, AUG - 2), (0, 0))
    ).astype(LOW)

    half = HEAD_DIM // 2
    frequency = 1000.0 ** (-(jnp.arange(half, dtype=WIDE) * 2.0) / HEAD_DIM)
    angles = own_places.astype(WIDE)[None] * frequency[:, None]
    cosine, sine = jnp.cos(angles), jnp.sin(angles)

    kv = project(qkv_t, x, cosine, sine, "kv", 1)
    members = 2 * near
    if members == 2:
        kvs = [kv, lax.ppermute(kv, "core", SWAP)]
        other_second = lax.dynamic_index_in_dim(second, 1 - member, 0, False)
        kas = [key_aug(own_second), key_aug(other_second)]
        types = [WIDE, LOW]
    else:
        kvs = [lax.all_gather(kv, ("zm", "core"), axis=1, tiled=True)]
        kas = [key_aug(second.reshape(-1))]
        types = [LOW]
    q = project(qkv_t, x, cosine, sine, "q", 0)
    spans = [(i * HEADS // PIECES, HEADS // PIECES) for i in range(PIECES)]
    top_parts = bring(out_grad, tuple(far(kv)))
    attended, lse = attend_forward(q, query_aug, kvs, kas, (), 0, HEADS)
    grad_top = stack(top_parts, tuple(far(attended)))

    (x_low, hidden, gug, mix_grad, d_resid_one, proj_grad, att_grad, sums), output = middle(
        attended, x, grad_top, pack, small, rows
    )
    returned = send_back(output[:1], 0)

    def ungroup(g):
        g = g.reshape(blocks, width, tp // blocks, units).swapaxes(1, 2)
        return g.reshape(tp, dp, width // dp, units)

    if merged:
        mine, send = side_grads(core, mix_grad, hidden, proj_grad, [attended], sums, width // dp + no + 8, chips)
    else:
        g_out = dot(proj_grad, attended, 0, 1).astype(LOW).reshape(dp, tp, no, width)
        spread_sums = jnp.broadcast_to(sums.astype(LOW), (dp, tp, 8, width))
        side = collapse_all(jnp.concatenate([g_out, spread_sums], axis=2).swapaxes(0, 1))
        g_down = jnp.einsum("td,jtf->jdf", mix_grad, hidden, preferred_element_type=WIDE).astype(LOW)
        g_down = collapse_all(ungroup(g_down))
        mine = mix_grad
    split = blocks // 2
    g_gu = gate_up_grads(x_low, gug, 0, split, (), (mine,), dp)
    held = ()
    if merged:
        held = collapse_core(mine, send, 1, tuple(far(g_gu)))
    g_gu = gate_up_grads(x_low, gug, split, blocks - split, (g_gu,), tuple(held), dp)
    g_gu = g_gu.reshape(dp, blocks, width // dp, 2, tp // blocks, units).transpose(0, 1, 4, 2, 3, 5)
    g_gu = g_gu.reshape(dp, tp, width // dp, 2 * units)
    shared_gu = lax.psum_scatter(g_gu, ("chip", "core"), scatter_dimension=0, tiled=False)
    shared_gu = lax.psum_scatter(shared_gu, flat, scatter_dimension=0, tiled=False).astype(WIDE)
    spans = [(i * HEADS // PIECES, HEADS // PIECES) for i in range(PIECES)]

    dqs, grads, parts = [], [], []
    for i, (start, count) in enumerate(spans):
        after = tuple(held) + (tuple(far(g_gu)) if i == 0 else ()) + (tuple(far(*returned[i - 1 : i])) if i in (1, 2) else ())
        dq, dkv = attend_backward(q, att_grad, attended, lse, query_aug, kvs, kas, types, after, start, count)
        if i == 0:
            returned += send_back([stack([part], (dq,)) for part in output[1:]], 1)
        if merged and i == 0:
            held = collapse_far(*held, (dq,))
        if merged and i == 1:
            held = collapse_near(*held, (dq,))
        if merged and i == 2:
            total = collapse_z(held)
            held = (total,)
        if members == 2:
            own_dkv, others = dkv[0], (lax.ppermute(dkv[1], "core", SWAP),)
        else:
            summed = lax.psum_scatter(dkv[0], ("zm", "core"), scatter_dimension=2, tiled=True)
            own_dkv, others = summed.astype(WIDE), ()
        dqs.append((dq, own_dkv, others))
    for i, (dq, own_dkv, others) in enumerate(dqs):
        grad, part = unturn(dq, own_dkv, others, cosine, sine, x, ())
        grads.append(grad)
        parts.append(part)
    if merged:
        g_down, side = total[: width // dp], total[width // dp :]
    g_qkv = jnp.concatenate(parts, axis=1).reshape(dp, tp, nq, width)
    if not by_hand:
        g_qkv = collapse_all(g_qkv.swapaxes(0, 1))
        in_grad = finish(grads, d_resid_one, qkv_t, (), 0, own)
        sent = [in_grad[k * piece : (k + 1) * piece] for k in range(rows)]
        in_grad = give_back(sent)
    else:
        g_qkv = g_qkv.reshape(chips, 2, tp, nq, width)
        mine, send = pick(g_qkv, core, 1), pick(g_qkv, 1 - core, 1)
        in_grad = [finish(grads, d_resid_one, qkv_t, (send,), 0, piece)]
        held = collapse_core(mine, send, 0, (in_grad[0],))
        for k in range(1, rows):
            in_grad.append(finish(grads, d_resid_one, qkv_t, (held[0],), k, piece))
        held = collapse_far(*held, (in_grad[-1],))
        g_qkv = collapse_z(collapse_near(*held))
        sent = in_grad
        in_grad = give_back(in_grad)
    vector_grads = lax.dynamic_slice_in_dim(side[no : no + 4], mine_at, no, 1)
    order = jnp.stack([(r - z) % rows for r in range(rows)]).astype(jnp.int32)
    return (
        settle_late(returned, order, tuple(far(sent[-1]))),
        in_grad,
        g_qkv.T,
        side[:no].T,
        vector_grads[0],
        vector_grads[1],
        shared_gu[:, :units],
        shared_gu[:, units:],
        g_down.T,
        vector_grads[2],
        vector_grads[3],
    )


def solution(mesh):
    dp, tp = mesh.shape["dp"], mesh.shape["tp"]

    def run(*arrays):
        rows = arrays[0].shape[0] // dp
        groups = 2 * rows
        grid = Mesh(
            mesh.devices.reshape(dp // 2, 2, groups, tp // groups), ("chip", "core", "zg", "zm")
        )
        d, t = ("chip", "core"), ("zg", "zm")
        both = d + t
        placed = (
            P(d, t, None),
            P(d, None),
            P(d, None),
            P(None, both),
            P(None, both),
            P(both),
            P(both),
            P(d, t),
            P(d, t),
            P(t, d),
            P(both),
            P(both),
            P(d, t, None),
        )
        return jax.shard_map(
            functools.partial(local, tp, (dp // 2, groups)),
            mesh=grid,
            in_specs=placed,
            out_specs=(
                P(d, t, None),
                P(d, t, None),
                P(None, both),
                P(None, both),
                P(both),
                P(both),
                P(d, t),
                P(d, t),
                P(t, d),
                P(both),
                P(both),
            ),
            check_vma=False,
        )(*arrays)

    return run
```
